128 devices in a mesh: det: 16 (over x_hi, z, core), frames: 8 (over y, x_lo).
Axes of the slice: x: 4 (x_hi: 2, x_lo: 2; x = x_hi * 2 + x_lo), y: 4, z: 4, core: 2. Of those that a mesh axis runs over, the one named last changes fastest.
Arguments:
- probe: bfloat16 [2, 2048, 2048], P(None, 'det'), may hold values from -6 to 6
- object_field: bfloat16 [2, 2048, 2304], P(None, 'det'), may hold values from -4 to 4
- positions: int32 [8], P('frames'), may hold values from 0 to 256, as said below
- cotangent: bfloat16 [8, 2048, 2048], P('frames', 'det'), may hold values from -6 to 6
- kernel: float32 [57, 57], replicated, may hold values from 0 to 0.03508772
Outputs:
- wave_grad: bfloat16 [2, 8, 2048, 2048], P(None, 'frames', 'det')
- kernel_grad: float32 [57, 57], replicated
The draws below stay inside these ranges and needn't reach their ends.
Inputs may be any that keep to these rules, and one draw needn't show every extreme that they name: positions[f] is the first object column of frame f's window; some frame starts at 0 and some at 256.
All inputs are finite; a program needn't handle non-finite values.
Results may differ from the reference program's by a relative error of at most 0.011.
Values may be sent and summed in bfloat16 or wider, within the bound.
A program may use at most 128 MiB of HBM per device.

```python
import math
import jax
import jax.numpy as jnp
from jax import lax

N = 2048
HK = 28
SPAN = 256
FRAMES = 8


def draw_positions(key, part):
    key = jax.random.fold_in(key, 7)
    first_key, second_key, third_key = jax.random.split(key, 3)
    offsets = jax.random.randint(first_key, (FRAMES,), 0, SPAN + 1, dtype=jnp.int32)
    lowest_at = jax.random.randint(second_key, (), 0, FRAMES, dtype=jnp.int32)
    distance = jax.random.randint(third_key, (), 1, FRAMES, dtype=jnp.int32)
    highest_at = (lowest_at + distance) % FRAMES
    slots = jnp.arange(FRAMES, dtype=jnp.int32)
    offsets = jnp.where(slots == lowest_at, 0, offsets)
    return jnp.where(slots == highest_at, SPAN, offsets).astype(jnp.int32)


def levels(own_key, dims, shards, low, largest):
    factor_of, own = 1.0, jax.random.fold_in(own_key, 6)
    for dim, parts in shards:
        heights = jnp.exp(jax.random.uniform(jax.random.fold_in(own, dim), (parts,), jnp.float32, low / len(shards), largest / len(shards)))
        factor_of = factor_of * jnp.repeat(heights, dims[dim] // parts).reshape([-1 if axis == dim else 1 for axis in range(len(dims))])
    return factor_of


def bell_draw(stream_key, shape, scale, most, shards=(), kind=jnp.bfloat16):
    result = scale * jax.random.normal(stream_key, shape, jnp.float32)
    if shards:
        result = result * levels(stream_key, shape, shards, -0.22, 0.18)
    return jnp.clip(result, -most, most).astype(kind)


def setup_inputs(seed: int = 0) -> dict:
    arg_keys = jax.random.split(jax.random.key(seed), 6)
    return {
        "probe": bell_draw(arg_keys[0], (2, N, N), 1.0, 6.0, ((1, 16),)),
        "object_field": bell_draw(arg_keys[1], (2, N, N + SPAN), 0.7, 4.0, ((1, 16),)),
        "positions": draw_positions(jax.random.fold_in(arg_keys[5], 71), 0),
        "cotangent": bell_draw(arg_keys[3], (FRAMES, N, N), 1.0, 6.0, ((0, 8), (1, 16))),
        "kernel": jnp.clip(jax.random.uniform(arg_keys[4], (2 * HK + 1, 2 * HK + 1), jnp.float32, 0.0, 0.03508772), 0.0, 0.03508772),
    }


def dft_tables(extent):
    indices = jnp.arange(extent, dtype=jnp.int32)
    product = indices[:, None] * indices[None, :] % extent
    phase_angle = product.astype(jnp.float32) * (2.0 * math.pi / extent)
    table_scale = 1.0 / math.sqrt(extent)
    cosine = (jnp.cos(phase_angle) * table_scale).astype(jnp.bfloat16)
    sine = (jnp.sin(phase_angle) * table_scale).astype(jnp.bfloat16)
    return (cosine, sine)

def band_stack(kernel, width):
    tap_count = kernel.shape[0]
    kernel_reach = tap_count - 1
    outer_index = jnp.arange(width + kernel_reach, dtype=jnp.int32)
    inner_index = jnp.arange(width, dtype=jnp.int32)
    lag_index = jnp.arange(tap_count, dtype=jnp.int32)
    band_marks = (outer_index[:, None, None] - inner_index[None, :, None] == lag_index[None, None, :]).astype(jnp.float32)
    rounded = lax.optimization_barrier(kernel.astype(jnp.bfloat16)).astype(jnp.float32)
    across = jnp.einsum('ij,zyj->izy', rounded, band_marks, precision=lax.Precision.HIGHEST).astype(jnp.bfloat16)
    downward = jnp.einsum('ij,zyi->jyz', rounded, band_marks, precision=lax.Precision.HIGHEST).astype(jnp.bfloat16)
    return (across, downward)

def band_sums(products, tap_count):
    group_size, local_rows, extent = products.shape
    flattened = products.reshape(group_size, local_rows * extent)
    flattened = jnp.pad(flattened, ((0, 0), (0, local_rows)))
    skewed = flattened.reshape(group_size, local_rows, extent + 1)
    return lax.optimization_barrier(jnp.sum(skewed[:, :, :tap_count], axis=1))

def stored(value):
    return lax.optimization_barrier(value.astype(jnp.bfloat16))

def exact(left, right):
    return jnp.dot(left.astype(jnp.float32), right.astype(jnp.float32), precision=lax.Precision.HIGHEST)

def correlate(intensity, frame_cot, across, block_width):
    extent = frame_cot.shape[0]
    tap_count = across.shape[0]
    kernel_reach = (tap_count - 1) // 2
    padded = jnp.pad(frame_cot, kernel_reach, mode='wrap')
    block_count = extent // block_width
    starts = jnp.arange(block_count, dtype=jnp.int32) * block_width
    column_blocks = jax.vmap(lambda first_col: lax.dynamic_slice_in_dim(padded, first_col, block_width + 2 * kernel_reach, 1))(starts)
    intensity_blocks = intensity.astype(jnp.float32).reshape(extent, block_count, block_width).transpose(1, 0, 2)

    def per_tap(gradient, tap_index):
        shifted = lax.dynamic_slice_in_dim(column_blocks, tap_index, extent, 1).astype(jnp.float32)
        weights = lax.dynamic_index_in_dim(across, tap_index, 0, keepdims=False).astype(jnp.float32)
        gradient = gradient + jnp.einsum('bnz,zy->bny', shifted, weights, precision=lax.Precision.HIGHEST)
        products = jnp.einsum('bny,bnz->yz', intensity_blocks, shifted, precision=lax.Precision.HIGHEST)
        return (gradient, band_sums(products[None], tap_count)[0])
    start_value = jnp.zeros((block_count, extent, block_width), jnp.float32)
    gradient, lag_sums = lax.scan(per_tap, start_value, jnp.arange(tap_count, dtype=jnp.int32))
    gradient = gradient.transpose(1, 0, 2).reshape(extent, extent)
    return (gradient, lag_sums)

def reference(probe, object_field, positions, cotangent, kernel):
    cosine, sine = dft_tables(N)
    block_width = 128 if N % 128 == 0 else N
    across, downward = band_stack(kernel, block_width)
    probe_re = probe[0].astype(jnp.float32)
    probe_im = probe[1].astype(jnp.float32)

    def frame_pass(inputs):
        column_start, frame_cot = inputs
        window = lax.dynamic_slice_in_dim(object_field, column_start.astype(jnp.int32), N, 2).astype(jnp.float32)
        wave_re = stored(probe_re * window[0] - probe_im * window[1])
        wave_im = stored(probe_re * window[1] + probe_im * window[0])
        half_re = stored(exact(wave_re, cosine) + exact(wave_im, sine))
        half_im = stored(exact(wave_im, cosine) - exact(wave_re, sine))
        spec_re = exact(cosine, half_re) + exact(sine, half_im)
        spec_im = exact(cosine, half_im) - exact(sine, half_re)
        intensity = stored(spec_re * spec_re + spec_im * spec_im)
        gradient, lag_sums = correlate(intensity, frame_cot, across, block_width)
        grad_wide = stored(gradient).astype(jnp.float32)
        weight_re = stored(2.0 * grad_wide * spec_re)
        weight_im = stored(2.0 * grad_wide * spec_im)
        back_re = stored(exact(cosine, weight_re) - exact(sine, weight_im))
        back_im = stored(exact(cosine, weight_im) + exact(sine, weight_re))
        out_re = (exact(back_re, cosine) - exact(back_im, sine)).astype(jnp.bfloat16)
        out_im = (exact(back_im, cosine) + exact(back_re, sine)).astype(jnp.bfloat16)
        return (jnp.stack([out_re, out_im]), lag_sums)
    waves, lag_sums = lax.map(frame_pass, (positions, cotangent))
    wave_grad = jnp.transpose(waves, (1, 0, 2, 3))
    kernel_grad = lax.optimization_barrier(jnp.sum(lag_sums, axis=0)) / (FRAMES * N)
    return (wave_grad, kernel_grad)
```

```python
import functools
import math

import jax
import jax.numpy as jnp
import ml_dtypes
import numpy as np
from jax import lax
from jax.experimental import pallas as pl
from jax.experimental.pallas import tpu as pltpu
from jax.sharding import PartitionSpec as P

MESH = pl.DeviceIdType.MESH
F32, BF16 = jnp.float32, jnp.bfloat16
N = 2048
HK = 28
TAPS = 2 * HK + 1
RADIX = 8
SUB = N // RADIX
BLK = 128
DET = N // BLK
ROOT_HALF = math.sqrt(0.5)


def as_bf16(values):
    return np.asarray(values, np.float32).astype(ml_dtypes.bfloat16)


@functools.cache
def tables():
    residue = np.arange(RADIX)[:, None, None]
    point = np.arange(SUB)[None, :, None]
    freq = np.arange(SUB)[None, None, :]
    angle = 2 * np.pi * (point * (RADIX * freq + residue) % N) / N
    cos, sin = np.cos(angle) / math.sqrt(N), np.sin(angle) / math.sqrt(N)
    forward = np.concatenate(
        [np.concatenate([cos, -sin], 2), np.concatenate([sin, cos], 2)], 1
    )
    inverse = np.swapaxes(forward, 1, 2)

    spread = np.zeros((1024, 1024))
    for r in range(RADIX):
        spread[RADIX * np.arange(BLK) + r, BLK * r + np.arange(BLK)] = 1

    lag = np.arange(64)
    ky = RADIX * np.arange(SUB)[None, :, None] + residue
    beta = 2 * np.pi * (ky * (lag[None, None, :] - HK) % N) / N
    used = (lag < TAPS)[None, None, :]
    cos, sin = np.cos(beta) * used, np.sin(beta) * used
    row_lags = np.concatenate(
        [np.concatenate([cos, -sin], 2), np.concatenate([sin, cos], 2)], 1
    )

    alpha = 2 * np.pi * (np.arange(BLK) + 0.5) / 256
    lane = np.arange(64)
    halo_u = np.where(lane < HK, lane, lane - HK + HK + BLK)
    halo_on = lane < 2 * HK
    u = np.concatenate([np.arange(BLK) + HK, halo_u, halo_u])
    on = np.concatenate([np.ones(BLK, bool), halo_on, halo_on])
    phase = alpha[:, None] * u[None, :]
    across = np.concatenate([np.cos(phase) * on, -np.sin(phase) * on], 0) / 16

    order = (RADIX * np.arange(16)[None, :] + np.arange(RADIX)[:, None]).reshape(-1)
    phase = alpha[:, None] * (order + HK)[None, :]
    across_own = np.concatenate([np.cos(phase), -np.sin(phase)], 0) / 16
    across_back = 2 * across_own.T

    pick = np.zeros((512, BLK))
    t = np.arange(HK)
    pick[BLK - HK + t, t] = 1
    pick[BLK + t, HK + t] = 1
    pick[256 + BLK - HK + t, 64 + t] = 1
    pick[384 + t, 64 + HK + t] = 1

    tap = np.arange(BLK)
    phase = alpha[:, None] * (tap - HK)[None, :]
    on = tap < TAPS
    kernel_x = np.concatenate([np.cos(phase) * on, np.sin(phase) * on], 1)
    tap = np.arange(BLK) % 64
    phase = alpha[:, None] * (tap - HK)[None, :]
    on = tap < TAPS
    lag_x = 2 * np.stack([np.cos(phase) * on, np.sin(phase) * on])
    return dict(
        forward=as_bf16(forward),
        inverse=as_bf16(inverse),
        spread=as_bf16(spread),
        row_lags=as_bf16(row_lags),
        across=as_bf16(across),
        across_own=as_bf16(across_own),
        across_back=as_bf16(across_back),
        pick=as_bf16(pick),
        eye=as_bf16(np.eye(BLK)),
        kernel_x=kernel_x.astype(np.float32),
        lag_x=lag_x.astype(np.float32),
    )


def dot(a, b):
    return jnp.dot(a, b, preferred_element_type=F32)


def dot_t(a, b):
    return lax.dot_general(a, b, (((1,), (1,)), ((), ())), preferred_element_type=F32)


def add(a, b):
    return (a[0] + b[0], a[1] + b[1])


def sub(a, b):
    return (a[0] - b[0], a[1] - b[1])


def dft4(z, sign):
    c0, c1 = add(z[0], z[2]), sub(z[0], z[2])
    d0, t = add(z[1], z[3]), sub(z[1], z[3])
    d1 = (-t[1], t[0]) if sign > 0 else (t[1], -t[0])
    return [add(c0, d0), add(c1, d1), sub(c0, d0), sub(c1, d1)]


def dft8(z, sign):
    a = [add(z[q], z[q + 4]) for q in range(4)]
    b = [sub(z[q], z[q + 4]) for q in range(4)]
    if sign > 0:
        b[1] = (ROOT_HALF * (b[1][0] - b[1][1]), ROOT_HALF * (b[1][1] + b[1][0]))
        b[2] = (-b[2][1], b[2][0])
        b[3] = (-ROOT_HALF * (b[3][0] + b[3][1]), ROOT_HALF * (b[3][0] - b[3][1]))
    else:
        b[1] = (ROOT_HALF * (b[1][0] + b[1][1]), ROOT_HALF * (b[1][1] - b[1][0]))
        b[2] = (b[2][1], -b[2][0])
        b[3] = (ROOT_HALF * (b[3][1] - b[3][0]), -ROOT_HALF * (b[3][1] + b[3][0]))
    even, odd = dft4(a, sign), dft4(b, sign)
    return [half for pair in zip(even, odd) for half in pair]


def split_residues(source, target):
    def body(step, carry):
        rows = pl.ds(pl.multiple_of(step * 16, 16), 16)
        for p in range(2):
            z = [
                tuple(source[2 * q + p, c, rows, :].astype(F32) for c in range(2))
                for q in range(RADIX)
            ]
            out = dft8(z, -1)
            for r in range(RADIX):
                for c in range(2):
                    first = c * SUB + p * BLK
                    target[r, rows, first : first + BLK] = out[r][c].astype(BF16)
        return carry

    lax.fori_loop(0, BLK // 16, body, 0)


def join_residues(source, store):
    def body(step, carry):
        rows = pl.ds(pl.multiple_of(step * 16, 16), 16)
        for p in range(2):
            z = [
                tuple(
                    source[r, rows, c * SUB + p * BLK : c * SUB + (p + 1) * BLK]
                    for c in range(2)
                )
                for r in range(RADIX)
            ]
            out = dft8(z, 1)
            for q in range(RADIX):
                for c in range(2):
                    store(2 * q + p, c, step, out[q][c].astype(BF16))
        return carry

    lax.fori_loop(0, BLK // 16, body, 0)


def loop(count, body):
    def step(index, carry):
        body(index)
        return carry

    lax.fori_loop(0, count, step, 0)


def kernel_body(
    frames,
    pos_ref, probe_ref, object_ref, cot_ref, taps_ref,
    across_ref, own_ref, back_ref, pick_ref, eye_ref, kx_ref, lagx_ref,
    fwd_hbm, inv_hbm, spread_hbm, lags_hbm,
    wave_ref, kgrad_ref,
    fwd, inv, spread, lags,
    cot_main, cot_halo, halo_out, wide, parts, sums, chat,
    half_out, half_in, back_out, back_in,
    ig_x, ig_nat, ig_perm, inten, inten_nat, tap_pad,
    kg_own, kg_frames, kg_det,
    table_sem, main_send, main_recv, halo_send, halo_recv,
    half_send, half_recv, back_send, back_recv, kgf_send, kgf_recv, kgd_send, kgd_recv,
):
    me = lax.axis_index("det")
    my_frame = lax.axis_index("frames")
    loads = [
        pltpu.make_async_copy(source, target, table_sem.at[index])
        for index, (source, target) in enumerate(
            ((inv_hbm, inv), (fwd_hbm, fwd), (lags_hbm, lags), (spread_hbm, spread))
        )
    ]
    for load in loads:
        load.start()

    def det_peer(offset):
        return lax.rem(me + offset, DET)

    def frame_peer(offset):
        return lax.rem(my_frame + offset, frames)

    barrier = pltpu.get_barrier_semaphore()
    loop(DET - 1, lambda o: pl.semaphore_signal(
        barrier, inc=1, device_id={"det": det_peer(o + 1)}, device_id_type=MESH))
    if frames > 1:
        loop(frames - 1, lambda o: pl.semaphore_signal(
            barrier, inc=1, device_id={"frames": frame_peer(o + 1)}, device_id_type=MESH))

    def exchange(source, target, send, recv):
        def copy(to, slot):
            return pltpu.make_async_remote_copy(
                src_ref=source(to),
                dst_ref=target.at[slot],
                send_sem=send.at[to],
                recv_sem=recv.at[slot],
                device_id={"det": to},
                device_id_type=MESH,
            )

        def start():
            loop(DET - 1, lambda o: copy(det_peer(o + 1), me).start())

        def wait_recv():
            loop(DET - 1, lambda o: copy(det_peer(o + 1), det_peer(o + 1)).wait_recv())

        def wait_send():
            loop(DET - 1, lambda o: copy(det_peer(o + 1), me).wait_send())

        return start, wait_recv, wait_send

    def lanes(block, width=BLK):
        return pl.ds(pl.multiple_of(block * width, width), width)

    main = exchange(lambda t: cot_ref.at[0, :, lanes(t)], cot_main, main_send, main_recv)
    halo = exchange(lambda t: halo_out.at[t], cot_halo, halo_send, halo_recv)
    half = exchange(lambda t: half_out.at[t], half_in, half_send, half_recv)
    back = exchange(lambda t: back_out.at[t], back_in, back_send, back_recv)

    def pack(block):
        before = lanes(lax.rem(block + DET - 1, DET))
        after = lanes(lax.rem(block + 1, DET))
        edges = jnp.concatenate(
            [
                cot_ref[0, rows, side]
                for rows in (pl.ds(0, 64), pl.ds(64, 64))
                for side in (before, after)
            ],
            axis=1,
        )
        halo_out[block] = dot(edges, pick_ref[...]).astype(BF16)

    loop(DET, pack)
    pl.semaphore_wait(barrier, DET - 1 + frames - 1)
    main[0]()
    halo[0]()

    position = pos_ref[0]
    distance = lax.broadcasted_iota(jnp.int32, (512, 256), 0) - lax.broadcasted_iota(
        jnp.int32, (512, 256), 1
    )
    shift = jnp.where(distance == position, 1.0, 0.0).astype(BF16)

    def exit_wave(q):
        wide_lanes = pl.ds(pl.multiple_of(q * 256, 256), 512)
        own = lanes(q, 256)
        w_re = dot(object_ref[0, :, wide_lanes], shift)
        w_im = dot(object_ref[1, :, wide_lanes], shift)
        p_re, p_im = probe_ref[0, :, own].astype(F32), probe_ref[1, :, own].astype(F32)
        re = (p_re * w_re - p_im * w_im).astype(BF16)
        im = (p_re * w_im + p_im * w_re).astype(BF16)
        for p in range(2):
            wide[2 * q + p, 0] = re[:, p * BLK : (p + 1) * BLK]
            wide[2 * q + p, 1] = im[:, p * BLK : (p + 1) * BLK]

    loop(RADIX, exit_wave)
    split_residues(wide, parts)
    loads[0].wait()

    def first_pass(r):
        out = dot_t(inv[r], parts[r]).astype(BF16).reshape(2, DET, 16, BLK)
        half_out[:, 0, lanes(r, 16), :] = out[0]
        half_out[:, 1, lanes(r, 16), :] = out[1]

    loop(RADIX, first_pass)
    half[0]()
    half_in[me] = half_out[me]

    tap_pad[...] = jnp.zeros_like(tap_pad)
    rounded = taps_ref[...].astype(BF16).astype(F32)
    tap_pad[0:TAPS, 0:TAPS] = rounded
    tap_pad[64 : 64 + TAPS, BLK : BLK + TAPS] = rounded
    tap_x = lax.dot_general(
        kx_ref[...], tap_pad[...], (((1,), (1,)), ((), ())),
        precision=lax.Precision.HIGHEST, preferred_element_type=F32,
    )
    tap_hi = tap_x.astype(BF16)
    tap_lo = (tap_x - tap_hi.astype(F32)).astype(BF16)

    cot_main[me] = cot_ref[0, :, lanes(me)]
    cot_halo[me] = halo_out[me]
    for load in loads[1:]:
        load.wait()
    main[1]()
    halo[1]()
    low = lax.broadcasted_iota(jnp.int32, (64, BLK), 1) < 64

    def cot_across(j):
        edge = cot_halo[j]
        zero = jnp.zeros_like(edge)
        spread_edge = jnp.concatenate(
            [jnp.where(low, edge, zero), jnp.where(low, zero, edge)], axis=0
        )
        both = jnp.concatenate([cot_main[j], spread_edge], axis=1)
        out = dot_t(across_ref[...], both).astype(BF16)
        wide[j, 0] = out[:BLK]
        wide[j, 1] = out[BLK:]

    loop(DET, cot_across)
    split_residues(wide, parts)

    def smooth(s):
        c = dot(parts[s], fwd[s])
        chat[s] = c
        k = dot_t(tap_hi, lags[s]) + dot_t(tap_lo, lags[s])
        c_re, c_im, k_re, k_im = c[:, :SUB], c[:, SUB:], k[:, :SUB], k[:, SUB:]
        g = jnp.concatenate(
            [c_re * k_re - c_im * k_im, c_re * k_im + c_im * k_re], axis=1
        )
        sums[s] = dot(g.astype(BF16), inv[s])

    loop(RADIX, smooth)

    def store_ig(block, c, step, value):
        rows = pl.ds(pl.multiple_of(c * BLK + step * 16, 16), 16)
        ig_x[rows, block * BLK : (block + 1) * BLK] = value

    join_residues(sums, store_ig)

    def ig_across(b):
        ig_nat[:, lanes(b, 256)] = dot(back_ref[...], ig_x[:, lanes(b, 256)]).astype(BF16)

    loop(RADIX, ig_across)
    for h in range(2):

        def to_residues(b, h=h):
            out = dot(ig_nat[:, h * 1024 : (h + 1) * 1024], spread[:, lanes(b, 256)])
            for p in range(2):
                ig_perm[2 * b + p, :, h * BLK : (h + 1) * BLK] = out[
                    :, p * BLK : (p + 1) * BLK
                ].astype(BF16)

        loop(4, to_residues)

    half[1]()
    split_residues(half_in, parts)

    def spectrum(r):
        x = dot(parts[r], fwd[r])
        re, im = x[:, :SUB], x[:, SUB:]
        intensity = (re * re + im * im).astype(BF16)
        for h in range(2):
            inten[h, :, lanes(r)] = intensity[:, h * BLK : (h + 1) * BLK]
        twice = 2.0 * ig_perm[r].astype(F32)
        grad = jnp.concatenate([(twice * re).astype(BF16), (twice * im).astype(BF16)], axis=1)
        sums[r] = dot(grad, inv[r])

    loop(RADIX, spectrum)

    def store_back(block, c, step, value):
        rows = pl.ds(pl.multiple_of(step * 16, 16), 16)
        back_out[block, c, rows, :] = value

    join_residues(sums, store_back)
    back[0]()
    back_in[me] = back_out[me]

    for h in range(2):

        def to_natural(b, h=h):
            out = dot_t(inten[h], spread[lanes(b, 256), :]).astype(BF16)
            inten_nat[:, pl.ds(pl.multiple_of(h * 1024 + b * 256, 256), 256)] = out

        loop(4, to_natural)

    def inten_across(b):
        out = dot(own_ref[...], inten_nat[:, lanes(b, 256)]).astype(BF16)
        for p in range(2):
            for c in range(2):
                wide[2 * b + p, c] = out[c * BLK : (c + 1) * BLK, p * BLK : (p + 1) * BLK]

    loop(RADIX, inten_across)
    split_residues(wide, parts)

    def lag_sums(s, total):
        x = dot(parts[s], fwd[s])
        c = chat[s]
        x_re, x_im, c_re, c_im = x[:, :SUB], x[:, SUB:], c[:, :SUB], c[:, SUB:]
        product = jnp.concatenate(
            [x_re * c_re + x_im * c_im, x_im * c_re - x_re * c_im], axis=1
        )
        return total + dot(product.astype(BF16), lags[s])

    by_lag = lax.fori_loop(0, RADIX, lag_sums, jnp.zeros((BLK, BLK), F32)).T
    kg = sum(
        lax.dot_general(
            by_lag[c * 64 : (c + 1) * 64], lagx_ref[c], (((1,), (0,)), ((), ())),
            precision=lax.Precision.HIGHEST, preferred_element_type=F32,
        )
        for c in range(2)
    ) * (1.0 / (frames * N))
    first = lax.broadcasted_iota(jnp.int32, (32, BLK), 1) < 64
    kg_own[0] = jnp.where(first, kg[:32], kg[32:])

    def frame_copy(to, slot):
        return pltpu.make_async_remote_copy(
            src_ref=kg_own.at[0],
            dst_ref=kg_frames.at[slot],
            send_sem=kgf_send.at[to],
            recv_sem=kgf_recv.at[slot],
            device_id={"frames": to},
            device_id_type=MESH,
        )

    if frames > 1:
        loop(frames - 1, lambda o: frame_copy(frame_peer(o + 1), my_frame).start())
    kg_frames[my_frame] = kg_own[0]
    if frames > 1:
        loop(frames - 1, lambda o: frame_copy(frame_peer(o + 1), frame_peer(o + 1)).wait_recv())
    kg_own[1] = sum(kg_frames[f] for f in range(frames))
    over_det = exchange(lambda t: kg_own.at[1], kg_det, kgd_send, kgd_recv)
    over_det[0]()
    kg_det[me] = kg_own[1]

    back[1]()

    def last_pass(r):
        turned = [
            dot_t(eye_ref[...], back_in[:, c, lanes(r, 16), :].reshape(SUB, BLK)).astype(BF16)
            for c in range(2)
        ]
        sums[r] = dot(jnp.concatenate(turned, axis=1), inv[r])

    loop(RADIX, last_pass)

    def store_wave(block, c, step, value):
        rows = pl.ds(pl.multiple_of(step * 16, 16), 16)
        wave_ref[c, 0, rows, block * BLK : (block + 1) * BLK] = value

    join_residues(sums, store_wave)

    over_det[1]()
    total = sum(kg_det[j] for j in range(DET))
    kgrad_ref[0:32, :] = total[:, 0:TAPS]
    kgrad_ref[32:TAPS, :] = pltpu.roll(total, 64, 1)[0 : TAPS - 32, 0:TAPS]

    for kind in (main, halo, half, back, over_det):
        kind[2]()
    if frames > 1:
        loop(frames - 1, lambda o: frame_copy(frame_peer(o + 1), my_frame).wait_send())


def on_device(frames, probe, object_field, positions, cotangent, kernel):
    t = tables()
    vmem = pl.BlockSpec(memory_space=pltpu.VMEM)
    hbm = pl.BlockSpec(memory_space=pl.ANY)
    small = [t[k] for k in ("across", "across_own", "across_back", "pick", "eye", "kernel_x", "lag_x")]
    large = [t[k] for k in ("forward", "inverse", "spread", "row_lags")]
    sem = pltpu.SemaphoreType.DMA
    scratch = [pltpu.VMEM(x.shape, BF16) for x in large] + [
        pltpu.VMEM((DET, BLK, BLK), BF16),
        pltpu.VMEM((DET, 64, BLK), BF16),
        pltpu.VMEM((DET, 64, BLK), BF16),
        pltpu.VMEM((DET, 2, BLK, BLK), BF16),
        pltpu.VMEM((RADIX, BLK, 2 * SUB), BF16),
        pltpu.VMEM((RADIX, BLK, 2 * SUB), F32),
        pltpu.VMEM((RADIX, BLK, 2 * SUB), F32),
        pltpu.VMEM((DET, 2, BLK, BLK), BF16),
        pltpu.VMEM((DET, 2, BLK, BLK), BF16),
        pltpu.VMEM((DET, 2, BLK, BLK), BF16),
        pltpu.VMEM((DET, 2, BLK, BLK), BF16),
        pltpu.VMEM((2 * BLK, N), BF16),
        pltpu.VMEM((BLK, N), BF16),
        pltpu.VMEM((RADIX, BLK, SUB), BF16),
        pltpu.VMEM((2, BLK, N // 2), BF16),
        pltpu.VMEM((BLK, N), BF16),
        pltpu.VMEM((BLK, 2 * BLK), F32),
        pltpu.VMEM((2, 32, BLK), F32),
        pltpu.VMEM((frames, 32, BLK), F32),
        pltpu.VMEM((DET, 32, BLK), F32),
        sem((4,)),
    ]
    scratch += [sem((DET,))] * 8 + [sem((frames,))] * 2 + [sem((DET,))] * 2
    return pl.pallas_call(
        functools.partial(kernel_body, frames),
        out_shape=(
            jax.ShapeDtypeStruct((2, 1, BLK, N), BF16),
            jax.ShapeDtypeStruct((TAPS, TAPS), F32),
        ),
        in_specs=[pl.BlockSpec(memory_space=pltpu.SMEM)] + [vmem] * 11 + [hbm] * 4,
        out_specs=(vmem, vmem),
        scratch_shapes=scratch,
        compiler_params=pltpu.CompilerParams(
            collective_id=0, has_side_effects=True, vmem_limit_bytes=56 * 1024 * 1024
        ),
        cost_estimate=pl.CostEstimate(flops=6_000_000_000, bytes_accessed=16_000_000, transcendentals=0),
    )(positions, probe, object_field, cotangent, kernel, *small, *large)


def solution(mesh):
    frames = mesh.shape["frames"]
    placed = (
        P(None, "det", None),
        P(None, "det", None),
        P("frames"),
        P("frames", "det", None),
        P(),
    )
    return jax.shard_map(
        functools.partial(on_device, frames),
        mesh=mesh,
        in_specs=placed,
        out_specs=(P(None, "frames", "det", None), P()),
        check_vma=False,
    )
```

```python
import functools
import math

import jax
import jax.numpy as jnp
import ml_dtypes
import numpy as np
from jax import lax
from jax.experimental import pallas as pl
from jax.experimental.pallas import tpu as pltpu
from jax.sharding import PartitionSpec as P

MESH = pl.DeviceIdType.MESH
F32, BF16 = jnp.float32, jnp.bfloat16
N = 2048
HK = 28
TAPS = 2 * HK + 1
RADIX = 8
SUB = N // RADIX
BLK = 128
DET = N // BLK
PARTS = 2
PART = BLK // PARTS
ROOT_HALF = math.sqrt(0.5)


def as_bf16(values):
    return np.asarray(values, np.float32).astype(ml_dtypes.bfloat16)


@functools.cache
def tables():
    residue = np.arange(RADIX)[:, None, None]
    point = np.arange(SUB)[None, :, None]
    freq = np.arange(SUB)[None, None, :]
    angle = 2 * np.pi * (point * (RADIX * freq + residue) % N) / N
    cos, sin = np.cos(angle) / math.sqrt(N), np.sin(angle) / math.sqrt(N)
    forward = np.concatenate(
        [np.concatenate([cos, -sin], 2), np.concatenate([sin, cos], 2)], 1
    )
    inverse = np.swapaxes(forward, 1, 2)

    spread = np.zeros((1024, 1024))
    for r in range(RADIX):
        spread[RADIX * np.arange(BLK) + r, BLK * r + np.arange(BLK)] = 1

    lag = np.arange(64)
    ky = RADIX * np.arange(SUB)[None, :, None] + residue
    beta = 2 * np.pi * (ky * (lag[None, None, :] - HK) % N) / N
    used = (lag < TAPS)[None, None, :]
    cos, sin = np.cos(beta) * used, np.sin(beta) * used
    row_lags = np.concatenate(
        [np.concatenate([cos, -sin], 2), np.concatenate([sin, cos], 2)], 1
    )

    alpha = 2 * np.pi * (np.arange(BLK) + 0.5) / 256
    lane = np.arange(64)
    halo_u = np.where(lane < HK, lane, lane - HK + HK + BLK)
    halo_on = lane < 2 * HK
    u = np.concatenate([np.arange(BLK) + HK, halo_u, halo_u])
    on = np.concatenate([np.ones(BLK, bool), halo_on, halo_on])
    phase = alpha[:, None] * u[None, :]
    across = np.concatenate([np.cos(phase) * on, -np.sin(phase) * on], 0) / 16

    order = (RADIX * np.arange(16)[None, :] + np.arange(RADIX)[:, None]).reshape(-1)
    phase = alpha[:, None] * (order + HK)[None, :]
    across_own = np.concatenate([np.cos(phase), -np.sin(phase)], 0) / 16
    across_back = 2 * across_own.T

    pick = np.zeros((512, BLK))
    t = np.arange(HK)
    pick[BLK - HK + t, t] = 1
    pick[BLK + t, HK + t] = 1
    pick[256 + BLK - HK + t, 64 + t] = 1
    pick[384 + t, 64 + HK + t] = 1

    tap = np.arange(BLK)
    phase = alpha[:, None] * (tap - HK)[None, :]
    on = tap < TAPS
    kernel_x = np.concatenate([np.cos(phase) * on, np.sin(phase) * on], 1)
    tap = np.arange(BLK) % 64
    phase = alpha[:, None] * (tap - HK)[None, :]
    on = tap < TAPS
    lag_x = 2 * np.stack([np.cos(phase) * on, np.sin(phase) * on])
    return dict(
        forward=as_bf16(forward),
        inverse=as_bf16(inverse),
        spread=as_bf16(spread),
        row_lags=as_bf16(row_lags),
        across=as_bf16(across),
        across_own=as_bf16(across_own),
        across_back=as_bf16(across_back),
        pick=as_bf16(pick),
        eye=as_bf16(np.eye(BLK)),
        kernel_x=kernel_x.astype(np.float32),
        lag_x=lag_x.astype(np.float32),
    )


def dot(a, b):
    return jnp.dot(a, b, preferred_element_type=F32)


def dot_t(a, b):
    return lax.dot_general(a, b, (((1,), (1,)), ((), ())), preferred_element_type=F32)


def add(a, b):
    return (a[0] + b[0], a[1] + b[1])


def sub(a, b):
    return (a[0] - b[0], a[1] - b[1])


def dft4(z, sign):
    c0, c1 = add(z[0], z[2]), sub(z[0], z[2])
    d0, t = add(z[1], z[3]), sub(z[1], z[3])
    d1 = (-t[1], t[0]) if sign > 0 else (t[1], -t[0])
    return [add(c0, d0), add(c1, d1), sub(c0, d0), sub(c1, d1)]


def dft8(z, sign):
    a = [add(z[q], z[q + 4]) for q in range(4)]
    b = [sub(z[q], z[q + 4]) for q in range(4)]
    if sign > 0:
        b[1] = (ROOT_HALF * (b[1][0] - b[1][1]), ROOT_HALF * (b[1][1] + b[1][0]))
        b[2] = (-b[2][1], b[2][0])
        b[3] = (-ROOT_HALF * (b[3][0] + b[3][1]), ROOT_HALF * (b[3][0] - b[3][1]))
    else:
        b[1] = (ROOT_HALF * (b[1][0] + b[1][1]), ROOT_HALF * (b[1][1] - b[1][0]))
        b[2] = (b[2][1], -b[2][0])
        b[3] = (ROOT_HALF * (b[3][1] - b[3][0]), -ROOT_HALF * (b[3][1] + b[3][0]))
    even, odd = dft4(a, sign), dft4(b, sign)
    return [half for pair in zip(even, odd) for half in pair]


def split_residues(source, target, start=0, count=BLK):
    def body(step, carry):
        rows = pl.ds(pl.multiple_of(start + step * 16, 16), 16)
        for p in range(2):
            z = [
                tuple(source[2 * q + p, c, rows, :].astype(F32) for c in range(2))
                for q in range(RADIX)
            ]
            out = dft8(z, -1)
            for r in range(RADIX):
                for c in range(2):
                    first = c * SUB + p * BLK
                    target[r, rows, first : first + BLK] = out[r][c].astype(BF16)
        return carry

    lax.fori_loop(0, count // 16, body, 0)


def join_residues(source, store, start=0, count=BLK):
    def body(step, carry):
        rows = pl.ds(pl.multiple_of(start + step * 16, 16), 16)
        for p in range(2):
            z = [
                tuple(
                    source[r, rows, c * SUB + p * BLK : c * SUB + (p + 1) * BLK]
                    for c in range(2)
                )
                for r in range(RADIX)
            ]
            out = dft8(z, 1)
            for q in range(RADIX):
                for c in range(2):
                    store(2 * q + p, c, start + step * 16, out[q][c].astype(BF16))
        return carry

    lax.fori_loop(0, count // 16, body, 0)


def loop(count, body, unroll=1):
    def step(index, carry):
        for part in range(unroll):
            body(index * unroll + part)
        return carry

    lax.fori_loop(0, count // unroll, step, 0)


def kernel_body(
    frames,
    pos_ref, probe_ref, object_ref, cot_ref, taps_ref,
    across_ref, own_ref, back_ref, pick_ref, eye_ref, kx_ref, lagx_ref,
    fwd_hbm, inv_hbm, spread_hbm, lags_hbm,
    wave_ref, kgrad_ref,
    fwd, inv, spread, lags,
    cot_main, cot_halo, halo_out, wide, parts, sums, chat,
    half_out, half_in, back_out, back_in,
    ig_x, ig_nat, ig_perm, inten, inten_nat, tap_pad,
    kg_own, kg_frames, kg_det,
    table_sem, main_send, main_recv, halo_send, halo_recv,
    half_send, half_recv, back_send, back_recv, kgf_send, kgf_recv, kgd_send, kgd_recv,
):
    me = lax.axis_index("det")
    my_frame = lax.axis_index("frames")
    loads = [
        pltpu.make_async_copy(source, target, table_sem.at[index])
        for index, (source, target) in enumerate(
            ((inv_hbm, inv), (fwd_hbm, fwd), (lags_hbm, lags), (spread_hbm, spread))
        )
    ]
    for load in loads:
        load.start()

    def det_peer(offset):
        return lax.rem(me + offset, DET)

    def frame_peer(offset):
        return lax.rem(my_frame + offset, frames)

    barrier = pltpu.get_barrier_semaphore()
    loop(DET - 1, lambda o: pl.semaphore_signal(
        barrier, inc=1, device_id={"det": det_peer(o + 1)}, device_id_type=MESH))
    if frames > 1:
        loop(frames - 1, lambda o: pl.semaphore_signal(
            barrier, inc=1, device_id={"frames": frame_peer(o + 1)}, device_id_type=MESH))

    def exchange(source, target, send, recv, part=0):
        def copy(to, slot):
            return pltpu.make_async_remote_copy(
                src_ref=source(to),
                dst_ref=target(slot),
                send_sem=send.at[part, to],
                recv_sem=recv.at[part, slot],
                device_id={"det": to},
                device_id_type=MESH,
            )

        def start():
            loop(DET - 1, lambda o: copy(det_peer(o + 1), me).start())

        def wait_recv():
            loop(DET - 1, lambda o: copy(det_peer(o + 1), det_peer(o + 1)).wait_recv())

        def wait_send():
            loop(DET - 1, lambda o: copy(det_peer(o + 1), me).wait_send())

        return start, wait_recv, wait_send

    def lanes(block, width=BLK):
        return pl.ds(pl.multiple_of(block * width, width), width)

    def by_parts(source, target, send, recv):
        return [
            exchange(
                lambda t, k=k: source.at[t, :, pl.ds(k * PART, PART), :],
                lambda t, k=k: target.at[t, :, pl.ds(k * PART, PART), :],
                send, recv, k,
            )
            for k in range(PARTS)
        ]

    main = exchange(
        lambda t: cot_ref.at[0, :, lanes(t)], lambda t: cot_main.at[t], main_send, main_recv
    )
    halo = exchange(lambda t: halo_out.at[t], lambda t: cot_halo.at[t], halo_send, halo_recv)
    half = by_parts(half_out, half_in, half_send, half_recv)
    back = by_parts(back_out, back_in, back_send, back_recv)

    def pack(block):
        before = lanes(lax.rem(block + DET - 1, DET))
        after = lanes(lax.rem(block + 1, DET))
        edges = jnp.concatenate(
            [
                cot_ref[0, rows, side]
                for rows in (pl.ds(0, 64), pl.ds(64, 64))
                for side in (before, after)
            ],
            axis=1,
        )
        halo_out[block] = dot(edges, pick_ref[...]).astype(BF16)

    loop(DET, pack, RADIX)
    pl.semaphore_wait(barrier, DET - 1 + frames - 1)
    main[0]()
    halo[0]()

    position = pos_ref[0]
    distance = lax.broadcasted_iota(jnp.int32, (512, 256), 0) - lax.broadcasted_iota(
        jnp.int32, (512, 256), 1
    )
    shift = jnp.where(distance == position, 1.0, 0.0).astype(BF16)

    def exit_wave(q):
        wide_lanes = pl.ds(pl.multiple_of(q * 256, 256), 512)
        own = lanes(q, 256)
        w_re = dot(object_ref[0, :, wide_lanes], shift)
        w_im = dot(object_ref[1, :, wide_lanes], shift)
        p_re, p_im = probe_ref[0, :, own].astype(F32), probe_ref[1, :, own].astype(F32)
        re = (p_re * w_re - p_im * w_im).astype(BF16)
        im = (p_re * w_im + p_im * w_re).astype(BF16)
        for p in range(2):
            wide[2 * q + p, 0] = re[:, p * BLK : (p + 1) * BLK]
            wide[2 * q + p, 1] = im[:, p * BLK : (p + 1) * BLK]

    loop(RADIX, exit_wave, RADIX)
    split_residues(wide, parts)
    loads[0].wait()

    def first_pass(r):
        out = dot_t(inv[r], parts[r]).astype(BF16).reshape(2, DET, 16, BLK)
        half_out[:, 0, lanes(r, 16), :] = out[0]
        half_out[:, 1, lanes(r, 16), :] = out[1]

    for k in range(PARTS):
        for r in range(k * RADIX // PARTS, (k + 1) * RADIX // PARTS):
            first_pass(r)
        half[k][0]()
    half_in[me] = half_out[me]

    tap_pad[...] = jnp.zeros_like(tap_pad)
    rounded = taps_ref[...].astype(BF16).astype(F32)
    tap_pad[0:TAPS, 0:TAPS] = rounded
    tap_pad[64 : 64 + TAPS, BLK : BLK + TAPS] = rounded
    tap_x = lax.dot_general(
        kx_ref[...], tap_pad[...], (((1,), (1,)), ((), ())),
        precision=lax.Precision.HIGHEST, preferred_element_type=F32,
    )
    tap_hi = tap_x.astype(BF16)
    tap_lo = (tap_x - tap_hi.astype(F32)).astype(BF16)

    cot_main[me] = cot_ref[0, :, lanes(me)]
    cot_halo[me] = halo_out[me]
    for load in loads[1:]:
        load.wait()
    main[1]()
    halo[1]()
    low = lax.broadcasted_iota(jnp.int32, (64, BLK), 1) < 64

    def cot_across(j):
        edge = cot_halo[j]
        zero = jnp.zeros_like(edge)
        spread_edge = jnp.concatenate(
            [jnp.where(low, edge, zero), jnp.where(low, zero, edge)], axis=0
        )
        both = jnp.concatenate([cot_main[j], spread_edge], axis=1)
        out = dot_t(across_ref[...], both).astype(BF16)
        wide[j, 0] = out[:BLK]
        wide[j, 1] = out[BLK:]

    loop(DET, cot_across, RADIX)
    split_residues(wide, parts)

    def smooth(s):
        c = dot(parts[s], fwd[s])
        chat[s] = c
        k = dot_t(tap_hi, lags[s]) + dot_t(tap_lo, lags[s])
        c_re, c_im, k_re, k_im = c[:, :SUB], c[:, SUB:], k[:, :SUB], k[:, SUB:]
        g = jnp.concatenate(
            [c_re * k_re - c_im * k_im, c_re * k_im + c_im * k_re], axis=1
        )
        sums[s] = dot(g.astype(BF16), inv[s])

    loop(RADIX, smooth, RADIX)

    def store_ig(block, c, row, value):
        rows = pl.ds(pl.multiple_of(c * BLK + row, 16), 16)
        ig_x[rows, block * BLK : (block + 1) * BLK] = value

    join_residues(sums, store_ig)

    def ig_across(b):
        ig_nat[:, lanes(b, 256)] = dot(back_ref[...], ig_x[:, lanes(b, 256)]).astype(BF16)

    loop(RADIX, ig_across, RADIX)
    for h in range(2):

        def to_residues(b, h=h):
            out = dot(ig_nat[:, h * 1024 : (h + 1) * 1024], spread[:, lanes(b, 256)])
            for p in range(2):
                ig_perm[2 * b + p, :, h * BLK : (h + 1) * BLK] = out[
                    :, p * BLK : (p + 1) * BLK
                ].astype(BF16)

        loop(4, to_residues, 4)

    def spectrum(r, rows):
        x = dot(parts[r, rows, :], fwd[r])
        re, im = x[:, :SUB], x[:, SUB:]
        intensity = (re * re + im * im).astype(BF16)
        for h in range(2):
            inten[h, rows, r * BLK : (r + 1) * BLK] = intensity[:, h * BLK : (h + 1) * BLK]
        twice = 2.0 * ig_perm[r, rows, :].astype(F32)
        grad = jnp.concatenate([(twice * re).astype(BF16), (twice * im).astype(BF16)], axis=1)
        sums[r, rows, :] = dot(grad, inv[r])

    def store_back(block, c, row, value):
        rows = pl.ds(pl.multiple_of(row, 16), 16)
        back_out[block, c, rows, :] = value

    for k in range(PARTS):
        half[k][1]()
        split_residues(half_in, parts, k * PART, PART)
        for r in range(RADIX):
            spectrum(r, slice(k * PART, (k + 1) * PART))
        join_residues(sums, store_back, k * PART, PART)
        back[k][0]()
    back_in[me] = back_out[me]

    for h in range(2):

        def to_natural(b, h=h):
            out = dot_t(inten[h], spread[lanes(b, 256), :]).astype(BF16)
            inten_nat[:, pl.ds(pl.multiple_of(h * 1024 + b * 256, 256), 256)] = out

        loop(4, to_natural, 4)

    def inten_across(b):
        out = dot(own_ref[...], inten_nat[:, lanes(b, 256)]).astype(BF16)
        for p in range(2):
            for c in range(2):
                wide[2 * b + p, c] = out[c * BLK : (c + 1) * BLK, p * BLK : (p + 1) * BLK]

    loop(RADIX, inten_across, RADIX)
    split_residues(wide, parts)

    def lag_sums(s, total):
        x = dot(parts[s], fwd[s])
        c = chat[s]
        x_re, x_im, c_re, c_im = x[:, :SUB], x[:, SUB:], c[:, :SUB], c[:, SUB:]
        product = jnp.concatenate(
            [x_re * c_re + x_im * c_im, x_im * c_re - x_re * c_im], axis=1
        )
        return total + dot(product.astype(BF16), lags[s])

    by_lag = jnp.zeros((BLK, BLK), F32)
    for s in range(RADIX):
        by_lag = lag_sums(s, by_lag)
    by_lag = by_lag.T
    kg = sum(
        lax.dot_general(
            by_lag[c * 64 : (c + 1) * 64], lagx_ref[c], (((1,), (0,)), ((), ())),
            precision=lax.Precision.HIGHEST, preferred_element_type=F32,
        )
        for c in range(2)
    ) * (1.0 / (frames * N))
    first = lax.broadcasted_iota(jnp.int32, (32, BLK), 1) < 64
    kg_own[0] = jnp.where(first, kg[:32], kg[32:])

    def frame_copy(to, slot):
        return pltpu.make_async_remote_copy(
            src_ref=kg_own.at[0],
            dst_ref=kg_frames.at[slot],
            send_sem=kgf_send.at[to],
            recv_sem=kgf_recv.at[slot],
            device_id={"frames": to},
            device_id_type=MESH,
        )

    if frames > 1:
        loop(frames - 1, lambda o: frame_copy(frame_peer(o + 1), my_frame).start())
    kg_frames[my_frame] = kg_own[0]
    if frames > 1:
        loop(frames - 1, lambda o: frame_copy(frame_peer(o + 1), frame_peer(o + 1)).wait_recv())
    kg_own[1] = sum(kg_frames[f] for f in range(frames))
    over_det = exchange(
        lambda t: kg_own.at[1], lambda t: kg_det.at[t], kgd_send, kgd_recv
    )
    over_det[0]()
    kg_det[me] = kg_own[1]

    def last_pass(r):
        turned = [
            dot_t(eye_ref[...], back_in[:, c, lanes(r, 16), :].reshape(SUB, BLK)).astype(BF16)
            for c in range(2)
        ]
        sums[r] = dot(jnp.concatenate(turned, axis=1), inv[r])

    for k in range(PARTS):
        back[k][1]()
        for r in range(k * RADIX // PARTS, (k + 1) * RADIX // PARTS):
            last_pass(r)

    def store_wave(block, c, row, value):
        rows = pl.ds(pl.multiple_of(row, 16), 16)
        wave_ref[c, 0, rows, block * BLK : (block + 1) * BLK] = value

    join_residues(sums, store_wave)

    over_det[1]()
    total = sum(kg_det[j] for j in range(DET))
    kgrad_ref[0:32, :] = total[:, 0:TAPS]
    kgrad_ref[32:TAPS, :] = pltpu.roll(total, 64, 1)[0 : TAPS - 32, 0:TAPS]

    for kind in (main, halo, *half, *back, over_det):
        kind[2]()
    if frames > 1:
        loop(frames - 1, lambda o: frame_copy(frame_peer(o + 1), my_frame).wait_send())


def hand_over(wave_in, kgrad_in, wave_out, kgrad_out, sems):
    copies = [
        pltpu.make_async_copy(wave_in, wave_out, sems.at[0]),
        pltpu.make_async_copy(kgrad_in, kgrad_out, sems.at[1]),
    ]
    for copy in copies:
        copy.start()
    for copy in copies:
        copy.wait()


def on_device(frames, probe, object_field, positions, cotangent, kernel):
    t = tables()
    vmem = pl.BlockSpec(memory_space=pltpu.VMEM)
    hbm = pl.BlockSpec(memory_space=pl.ANY)
    small = [t[k] for k in ("across", "across_own", "across_back", "pick", "eye", "kernel_x", "lag_x")]
    large = [t[k] for k in ("forward", "inverse", "spread", "row_lags")]
    sem = pltpu.SemaphoreType.DMA
    shapes = (
        jax.ShapeDtypeStruct((2, 1, BLK, N), BF16),
        jax.ShapeDtypeStruct((TAPS, TAPS), F32),
    )
    scratch = [pltpu.VMEM(x.shape, BF16) for x in large] + [
        pltpu.VMEM((DET, BLK, BLK), BF16),
        pltpu.VMEM((DET, 64, BLK), BF16),
        pltpu.VMEM((DET, 64, BLK), BF16),
        pltpu.VMEM((DET, 2, BLK, BLK), BF16),
        pltpu.VMEM((RADIX, BLK, 2 * SUB), BF16),
        pltpu.VMEM((RADIX, BLK, 2 * SUB), F32),
        pltpu.VMEM((RADIX, BLK, 2 * SUB), F32),
        pltpu.VMEM((DET, 2, BLK, BLK), BF16),
        pltpu.VMEM((DET, 2, BLK, BLK), BF16),
        pltpu.VMEM((DET, 2, BLK, BLK), BF16),
        pltpu.VMEM((DET, 2, BLK, BLK), BF16),
        pltpu.VMEM((2 * BLK, N), BF16),
        pltpu.VMEM((BLK, N), BF16),
        pltpu.VMEM((RADIX, BLK, SUB), BF16),
        pltpu.VMEM((2, BLK, N // 2), BF16),
        pltpu.VMEM((BLK, N), BF16),
        pltpu.VMEM((BLK, 2 * BLK), F32),
        pltpu.VMEM((2, 32, BLK), F32),
        pltpu.VMEM((frames, 32, BLK), F32),
        pltpu.VMEM((DET, 32, BLK), F32),
        sem((4,)),
    ]
    scratch += [sem((1, DET))] * 4 + [sem((PARTS, DET))] * 4
    scratch += [sem((frames,))] * 2 + [sem((1, DET))] * 2
    results = pl.pallas_call(
        functools.partial(kernel_body, frames),
        out_shape=shapes,
        in_specs=[pl.BlockSpec(memory_space=pltpu.SMEM)] + [vmem] * 11 + [hbm] * 4,
        out_specs=(vmem, vmem),
        scratch_shapes=scratch,
        compiler_params=pltpu.CompilerParams(
            collective_id=0, has_side_effects=True, vmem_limit_bytes=56 * 1024 * 1024
        ),
        cost_estimate=pl.CostEstimate(flops=6_000_000_000, bytes_accessed=16_000_000, transcendentals=0),
    )(positions, probe, object_field, cotangent, kernel, *small, *large)
    return pl.pallas_call(
        hand_over,
        out_shape=shapes,
        in_specs=[vmem] * 2,
        out_specs=(hbm, hbm),
        scratch_shapes=[sem((2,))],
    )(*results)


def solution(mesh):
    frames = mesh.shape["frames"]
    placed = (
        P(None, "det", None),
        P(None, "det", None),
        P("frames"),
        P("frames", "det", None),
        P(),
    )
    return jax.shard_map(
        functools.partial(on_device, frames),
        mesh=mesh,
        in_specs=placed,
        out_specs=(P(None, "frames", "det", None), P()),
        check_vma=False,
    )
```

```python
import functools
import math

import jax
import jax.numpy as jnp
import ml_dtypes
import numpy as np
from jax import lax
from jax.experimental import pallas as pl
from jax.experimental.pallas import tpu as pltpu
from jax.sharding import PartitionSpec as P

MESH = pl.DeviceIdType.MESH
F32, BF16 = jnp.float32, jnp.bfloat16
N = 2048
HK = 28
TAPS = 2 * HK + 1
RADIX = 8
SUB = N // RADIX
BLK = 128
DET = N // BLK
PARTS = 2
PART = BLK // PARTS
ROOT_HALF = math.sqrt(0.5)


def as_bf16(values):
    return np.asarray(values, np.float32).astype(ml_dtypes.bfloat16)


LOADED = (
    "cotangent", "pick", "object", "probe", "inverse", "taps", "kernel_x", "across",
    "forward", "row_lags", "across_back", "spread", "across_own", "lag_x", "eye",
)


@functools.cache
def tables():
    residue = np.arange(RADIX)[:, None, None]
    point = np.arange(SUB)[None, :, None]
    freq = np.arange(SUB)[None, None, :]
    angle = 2 * np.pi * (point * (RADIX * freq + residue) % N) / N
    cos, sin = np.cos(angle) / math.sqrt(N), np.sin(angle) / math.sqrt(N)
    forward = np.concatenate(
        [np.concatenate([cos, -sin], 2), np.concatenate([sin, cos], 2)], 1
    )
    inverse = np.swapaxes(forward, 1, 2)

    spread = np.zeros((1024, 1024))
    for r in range(RADIX):
        spread[RADIX * np.arange(BLK) + r, BLK * r + np.arange(BLK)] = 1

    lag = np.arange(64)
    ky = RADIX * np.arange(SUB)[None, :, None] + residue
    beta = 2 * np.pi * (ky * (lag[None, None, :] - HK) % N) / N
    used = (lag < TAPS)[None, None, :]
    cos, sin = np.cos(beta) * used, np.sin(beta) * used
    row_lags = np.concatenate(
        [np.concatenate([cos, -sin], 2), np.concatenate([sin, cos], 2)], 1
    )

    alpha = 2 * np.pi * (np.arange(BLK) + 0.5) / 256
    lane = np.arange(64)
    halo_u = np.where(lane < HK, lane, lane - HK + HK + BLK)
    halo_on = lane < 2 * HK
    u = np.concatenate([np.arange(BLK) + HK, halo_u, halo_u])
    on = np.concatenate([np.ones(BLK, bool), halo_on, halo_on])
    phase = alpha[:, None] * u[None, :]
    across = np.concatenate([np.cos(phase) * on, -np.sin(phase) * on], 0) / 16

    order = (RADIX * np.arange(16)[None, :] + np.arange(RADIX)[:, None]).reshape(-1)
    phase = alpha[:, None] * (order + HK)[None, :]
    across_own = np.concatenate([np.cos(phase), -np.sin(phase)], 0) / 16
    across_back = 2 * across_own.T

    pick = np.zeros((512, BLK))
    t = np.arange(HK)
    pick[BLK - HK + t, t] = 1
    pick[BLK + t, HK + t] = 1
    pick[256 + BLK - HK + t, 64 + t] = 1
    pick[384 + t, 64 + HK + t] = 1

    tap = np.arange(BLK)
    phase = alpha[:, None] * (tap - HK)[None, :]
    on = tap < TAPS
    kernel_x = np.concatenate([np.cos(phase) * on, np.sin(phase) * on], 1)
    tap = np.arange(BLK) % 64
    phase = alpha[:, None] * (tap - HK)[None, :]
    on = tap < TAPS
    lag_x = 2 * np.stack([np.cos(phase) * on, np.sin(phase) * on])
    return dict(
        forward=as_bf16(forward),
        inverse=as_bf16(inverse),
        spread=as_bf16(spread),
        row_lags=as_bf16(row_lags),
        across=as_bf16(across),
        across_own=as_bf16(across_own),
        across_back=as_bf16(across_back),
        pick=as_bf16(pick),
        eye=as_bf16(np.eye(BLK)),
        kernel_x=kernel_x.astype(np.float32),
        lag_x=lag_x.astype(np.float32),
    )


def dot(a, b):
    return jnp.dot(a, b, preferred_element_type=F32)


def dot_t(a, b):
    return lax.dot_general(a, b, (((1,), (1,)), ((), ())), preferred_element_type=F32)


def add(a, b):
    return (a[0] + b[0], a[1] + b[1])


def sub(a, b):
    return (a[0] - b[0], a[1] - b[1])


def dft4(z, sign):
    c0, c1 = add(z[0], z[2]), sub(z[0], z[2])
    d0, t = add(z[1], z[3]), sub(z[1], z[3])
    d1 = (-t[1], t[0]) if sign > 0 else (t[1], -t[0])
    return [add(c0, d0), add(c1, d1), sub(c0, d0), sub(c1, d1)]


def dft8(z, sign):
    a = [add(z[q], z[q + 4]) for q in range(4)]
    b = [sub(z[q], z[q + 4]) for q in range(4)]
    if sign > 0:
        b[1] = (ROOT_HALF * (b[1][0] - b[1][1]), ROOT_HALF * (b[1][1] + b[1][0]))
        b[2] = (-b[2][1], b[2][0])
        b[3] = (-ROOT_HALF * (b[3][0] + b[3][1]), ROOT_HALF * (b[3][0] - b[3][1]))
    else:
        b[1] = (ROOT_HALF * (b[1][0] + b[1][1]), ROOT_HALF * (b[1][1] - b[1][0]))
        b[2] = (b[2][1], -b[2][0])
        b[3] = (ROOT_HALF * (b[3][1] - b[3][0]), -ROOT_HALF * (b[3][1] + b[3][0]))
    even, odd = dft4(a, sign), dft4(b, sign)
    return [half for pair in zip(even, odd) for half in pair]


def split_residues(source, target, start=0, count=BLK):
    def body(step, carry):
        rows = pl.ds(pl.multiple_of(start + step * 16, 16), 16)
        for p in range(2):
            z = [
                tuple(source[2 * q + p, c, rows, :].astype(F32) for c in range(2))
                for q in range(RADIX)
            ]
            out = dft8(z, -1)
            for r in range(RADIX):
                for c in range(2):
                    first = c * SUB + p * BLK
                    target[r, rows, first : first + BLK] = out[r][c].astype(BF16)
        return carry

    lax.fori_loop(0, count // 16, body, 0)


def join_residues(source, store, start=0, count=BLK):
    def body(step, carry):
        rows = pl.ds(pl.multiple_of(start + step * 16, 16), 16)
        for p in range(2):
            z = [
                tuple(
                    source[r, rows, c * SUB + p * BLK : c * SUB + (p + 1) * BLK]
                    for c in range(2)
                )
                for r in range(RADIX)
            ]
            out = dft8(z, 1)
            for q in range(RADIX):
                for c in range(2):
                    store(2 * q + p, c, start + step * 16, out[q][c].astype(BF16))
        return carry

    lax.fori_loop(0, count // 16, body, 0)


def loop(count, body, unroll=1):
    def step(index, carry):
        for part in range(unroll):
            body(index * unroll + part)
        return carry

    lax.fori_loop(0, count // unroll, step, 0)


def kernel_body(
    frames,
    pos_ref, *refs,
):
    me = lax.axis_index("det")
    my_frame = lax.axis_index("frames")
    count = len(LOADED)
    sources, (wave_ref, kgrad_ref), held = refs[:count], refs[count : count + 2], refs[count + 2 :]
    held, rest = held[:count], held[count:]
    (
        cot_ref, pick_ref, object_ref, probe_ref, inv, taps_ref, kx_ref, across_ref,
        fwd, lags, back_ref, spread, own_ref, lagx_ref, eye_ref,
    ) = held
    (
        cot_main, cot_halo, halo_out, wide, parts, sums, chat,
        spec, half_out, half_in, back_out, back_in,
        ig_x, ig_nat, ig_perm, inten, inten_nat, tap_pad,
        kg_own, kg_frames, kg_sum, kg_det,
        load_sem, main_send, main_recv, halo_send, halo_recv,
        half_send, half_recv, back_send, back_recv,
        kgf_send, kgf_recv, kgd_send, kgd_recv,
    ) = rest

    def det_peer(offset):
        return lax.rem(me + offset, DET)

    def frame_peer(offset):
        return lax.rem(my_frame + offset, frames)

    barrier = pltpu.get_barrier_semaphore()
    loop(DET - 1, lambda o: pl.semaphore_signal(
        barrier, inc=1, device_id={"det": det_peer(o + 1)}, device_id_type=MESH))
    if frames > 1:
        loop(frames - 1, lambda o: pl.semaphore_signal(
            barrier, inc=1, device_id={"frames": frame_peer(o + 1)}, device_id_type=MESH))
    loads = {
        name: pltpu.make_async_copy(source, target, load_sem.at[index])
        for index, (name, source, target) in enumerate(zip(LOADED, sources, held))
    }
    for load in loads.values():
        load.start()

    def ready(*names):
        for name in names:
            loads[name].wait()


    def exchange(source, target, send, recv, part=0):
        def copy(to, slot):
            return pltpu.make_async_remote_copy(
                src_ref=source(to),
                dst_ref=target(slot),
                send_sem=send.at[part, to],
                recv_sem=recv.at[part, slot],
                device_id={"det": to},
                device_id_type=MESH,
            )

        def start():
            loop(DET - 1, lambda o: copy(det_peer(o + 1), me).start())

        def wait_recv():
            loop(DET - 1, lambda o: copy(det_peer(o + 1), det_peer(o + 1)).wait_recv())

        def wait_send():
            loop(DET - 1, lambda o: copy(det_peer(o + 1), me).wait_send())

        return start, wait_recv, wait_send

    def lanes(block, width=BLK):
        return pl.ds(pl.multiple_of(block * width, width), width)

    def by_parts(source, target, send, recv):
        return [
            exchange(
                lambda t, k=k: source.at[t, :, pl.ds(k * PART, PART), :],
                lambda t, k=k: target.at[t, :, pl.ds(k * PART, PART), :],
                send, recv, k,
            )
            for k in range(PARTS)
        ]

    main = exchange(
        lambda t: cot_ref.at[0, :, lanes(t)], lambda t: cot_main.at[t], main_send, main_recv
    )
    halo = exchange(lambda t: halo_out.at[t], lambda t: cot_halo.at[t], halo_send, halo_recv)
    half = by_parts(half_out, half_in, half_send, half_recv)
    back = by_parts(back_out, back_in, back_send, back_recv)

    def pack(block):
        before = lanes(lax.rem(block + DET - 1, DET))
        after = lanes(lax.rem(block + 1, DET))
        edges = jnp.concatenate(
            [
                cot_ref[0, rows, side]
                for rows in (pl.ds(0, 64), pl.ds(64, 64))
                for side in (before, after)
            ],
            axis=1,
        )
        halo_out[block] = dot(edges, pick_ref[...]).astype(BF16)

    ready("cotangent")
    pl.semaphore_wait(barrier, DET - 1 + frames - 1)
    main[0]()
    ready("pick")
    loop(DET, pack, RADIX)
    halo[0]()

    position = pos_ref[0]
    distance = lax.broadcasted_iota(jnp.int32, (512, 256), 0) - lax.broadcasted_iota(
        jnp.int32, (512, 256), 1
    )
    shift = jnp.where(distance == position, 1.0, 0.0).astype(BF16)

    def exit_wave(q):
        wide_lanes = pl.ds(pl.multiple_of(q * 256, 256), 512)
        own = lanes(q, 256)
        w_re = dot(object_ref[0, :, wide_lanes], shift)
        w_im = dot(object_ref[1, :, wide_lanes], shift)
        p_re, p_im = probe_ref[0, :, own].astype(F32), probe_ref[1, :, own].astype(F32)
        re = (p_re * w_re - p_im * w_im).astype(BF16)
        im = (p_re * w_im + p_im * w_re).astype(BF16)
        for p in range(2):
            wide[2 * q + p, 0] = re[:, p * BLK : (p + 1) * BLK]
            wide[2 * q + p, 1] = im[:, p * BLK : (p + 1) * BLK]

    ready("object", "probe")
    loop(RADIX, exit_wave, RADIX)
    split_residues(wide, parts)
    ready("inverse")

    def first_pass(r):
        out = dot_t(inv[r], parts[r]).astype(BF16).reshape(2, DET, 16, BLK)
        half_out[:, 0, lanes(r, 16), :] = out[0]
        half_out[:, 1, lanes(r, 16), :] = out[1]

    for k in range(PARTS):
        for r in range(k * RADIX // PARTS, (k + 1) * RADIX // PARTS):
            first_pass(r)
        if k == 0:
            main[2]()
            halo[2]()
        half[k][0]()
    half_in[me] = half_out[me]

    ready("taps", "kernel_x")
    tap_pad[...] = jnp.zeros_like(tap_pad)
    rounded = taps_ref[...].astype(BF16).astype(F32)
    tap_pad[0:TAPS, 0:TAPS] = rounded
    tap_pad[64 : 64 + TAPS, BLK : BLK + TAPS] = rounded
    tap_x = lax.dot_general(
        kx_ref[...], tap_pad[...], (((1,), (1,)), ((), ())),
        precision=lax.Precision.HIGHEST, preferred_element_type=F32,
    )
    tap_hi = tap_x.astype(BF16)
    tap_lo = (tap_x - tap_hi.astype(F32)).astype(BF16)

    cot_main[me] = cot_ref[0, :, lanes(me)]
    cot_halo[me] = halo_out[me]
    ready("across", "forward", "row_lags", "across_back", "spread", "across_own", "lag_x", "eye")
    main[1]()
    halo[1]()
    low = lax.broadcasted_iota(jnp.int32, (64, BLK), 1) < 64

    def cot_across(j):
        edge = cot_halo[j]
        zero = jnp.zeros_like(edge)
        spread_edge = jnp.concatenate(
            [jnp.where(low, edge, zero), jnp.where(low, zero, edge)], axis=0
        )
        both = jnp.concatenate([cot_main[j], spread_edge], axis=1)
        out = dot_t(across_ref[...], both).astype(BF16)
        wide[j, 0] = out[:BLK]
        wide[j, 1] = out[BLK:]

    loop(DET, cot_across, RADIX)
    split_residues(wide, parts)

    def smooth(s):
        c = dot(parts[s], fwd[s])
        chat[s] = c
        k = dot_t(tap_hi, lags[s]) + dot_t(tap_lo, lags[s])
        c_re, c_im, k_re, k_im = c[:, :SUB], c[:, SUB:], k[:, :SUB], k[:, SUB:]
        g = jnp.concatenate(
            [c_re * k_re - c_im * k_im, c_re * k_im + c_im * k_re], axis=1
        )
        sums[s] = dot(g.astype(BF16), inv[s])

    loop(RADIX, smooth, RADIX)

    def store_ig(block, c, row, value):
        rows = pl.ds(pl.multiple_of(c * BLK + row, 16), 16)
        ig_x[rows, block * BLK : (block + 1) * BLK] = value

    join_residues(sums, store_ig)

    def ig_across(b):
        ig_nat[:, lanes(b, 256)] = dot(back_ref[...], ig_x[:, lanes(b, 256)]).astype(BF16)

    loop(RADIX, ig_across, RADIX)
    for h in range(2):

        def to_residues(b, h=h):
            out = dot(ig_nat[:, h * 1024 : (h + 1) * 1024], spread[:, lanes(b, 256)])
            for p in range(2):
                ig_perm[2 * b + p, :, h * BLK : (h + 1) * BLK] = out[
                    :, p * BLK : (p + 1) * BLK
                ].astype(BF16)

        loop(4, to_residues, 4)

    def spectrum(r, rows):
        x = dot(parts[r, rows, :], fwd[r])
        re, im = x[:, :SUB], x[:, SUB:]
        intensity = (re * re + im * im).astype(BF16)
        for h in range(2):
            inten[h, rows, r * BLK : (r + 1) * BLK] = intensity[:, h * BLK : (h + 1) * BLK]
        spec[r, rows, :] = x

    def gradient(r, rows):
        x = spec[r, rows, :]
        re, im = x[:, :SUB], x[:, SUB:]
        twice = 2.0 * ig_perm[r, rows, :].astype(F32)
        grad = jnp.concatenate([(twice * re).astype(BF16), (twice * im).astype(BF16)], axis=1)
        sums[r, rows, :] = dot(grad, inv[r])

    def store_back(block, c, row, value):
        rows = pl.ds(pl.multiple_of(row, 16), 16)
        back_out[block, c, rows, :] = value

    def send_back(k):
        for r in range(RADIX):
            gradient(r, slice(k * PART, (k + 1) * PART))
        join_residues(sums, store_back, k * PART, PART)
        back[k][0]()

    for k in range(PARTS):
        half[k][1]()
        split_residues(half_in, parts, k * PART, PART)
        for r in range(RADIX):
            spectrum(r, slice(k * PART, (k + 1) * PART))
        if k < PARTS - 1:
            send_back(k)

    for h in range(2):

        def to_natural(b, h=h):
            out = dot_t(inten[h], spread[lanes(b, 256), :]).astype(BF16)
            inten_nat[:, pl.ds(pl.multiple_of(h * 1024 + b * 256, 256), 256)] = out

        loop(4, to_natural, 4)

    def inten_across(b):
        out = dot(own_ref[...], inten_nat[:, lanes(b, 256)]).astype(BF16)
        for p in range(2):
            for c in range(2):
                wide[2 * b + p, c] = out[c * BLK : (c + 1) * BLK, p * BLK : (p + 1) * BLK]

    loop(RADIX, inten_across, RADIX)
    split_residues(wide, parts)

    def lag_sums(s, total):
        x = dot(parts[s], fwd[s])
        c = chat[s]
        x_re, x_im, c_re, c_im = x[:, :SUB], x[:, SUB:], c[:, :SUB], c[:, SUB:]
        product = jnp.concatenate(
            [x_re * c_re + x_im * c_im, x_im * c_re - x_re * c_im], axis=1
        )
        return total + dot(product.astype(BF16), lags[s])

    by_lag = jnp.zeros((BLK, BLK), F32)
    for s in range(RADIX):
        by_lag = lag_sums(s, by_lag)
    by_lag = by_lag.T
    kg = sum(
        lax.dot_general(
            by_lag[c * 64 : (c + 1) * 64], lagx_ref[c], (((1,), (0,)), ((), ())),
            precision=lax.Precision.HIGHEST, preferred_element_type=F32,
        )
        for c in range(2)
    ) * (1.0 / (frames * N))
    first = lax.broadcasted_iota(jnp.int32, (32, BLK), 1) < 64
    kg_own[0] = jnp.where(first, kg[:32], kg[32:])

    def over_frames(source, target, send, recv):
        def copy(to, slot):
            return pltpu.make_async_remote_copy(
                src_ref=source(to),
                dst_ref=target.at[slot],
                send_sem=send.at[to],
                recv_sem=recv.at[slot],
                device_id={"frames": to},
                device_id_type=MESH,
            )

        def start():
            loop(frames - 1, lambda o: copy(frame_peer(o + 1), my_frame).start())

        def wait_recv():
            loop(frames - 1, lambda o: copy(frame_peer(o + 1), frame_peer(o + 1)).wait_recv())

        def wait_send():
            loop(frames - 1, lambda o: copy(frame_peer(o + 1), my_frame).wait_send())

        return start, wait_recv, wait_send

    across_frames = over_frames(lambda f: kg_own.at[0], kg_frames, kgf_send, kgf_recv)
    over_det = exchange(lambda t: kg_sum.at[0], lambda t: kg_det.at[t], kgd_send, kgd_recv)
    across_frames[0]()
    kg_frames[my_frame] = kg_own[0]
    send_back(PARTS - 1)
    back_in[me] = back_out[me]
    across_frames[1]()
    kg_sum[0] = sum(kg_frames[f] for f in range(frames))
    over_det[0]()
    kg_det[me] = kg_sum[0]

    def last_pass(r):
        turned = [
            dot_t(eye_ref[...], back_in[:, c, lanes(r, 16), :].reshape(SUB, BLK)).astype(BF16)
            for c in range(2)
        ]
        sums[r] = dot(jnp.concatenate(turned, axis=1), inv[r])

    for k in range(PARTS):
        back[k][1]()
        for r in range(k * RADIX // PARTS, (k + 1) * RADIX // PARTS):
            last_pass(r)

    def store_wave(block, c, row, value):
        rows = pl.ds(pl.multiple_of(row, 16), 16)
        wave_ref[c, 0, rows, block * BLK : (block + 1) * BLK] = value

    join_residues(sums, store_wave)

    over_det[1]()
    total = sum(kg_det[j] for j in range(DET))
    kgrad_ref[0:32, :] = total[:, 0:TAPS]
    kgrad_ref[32:TAPS, :] = pltpu.roll(total, 64, 1)[0 : TAPS - 32, 0:TAPS]

    for kind in (*half, *back, across_frames, over_det):
        kind[2]()


def hand_over(wave_in, kgrad_in, wave_out, kgrad_out, sems):
    copies = [
        pltpu.make_async_copy(wave_in, wave_out, sems.at[0]),
        pltpu.make_async_copy(kgrad_in, kgrad_out, sems.at[1]),
    ]
    for copy in copies:
        copy.start()
    for copy in copies:
        copy.wait()


def on_device(frames, probe, object_field, positions, cotangent, kernel):
    vmem = pl.BlockSpec(memory_space=pltpu.VMEM)
    hbm = pl.BlockSpec(memory_space=pl.ANY)
    arrays = dict(
        tables(), cotangent=cotangent, object=object_field, probe=probe, taps=kernel
    )
    arrays = [arrays[name] for name in LOADED]
    sem = pltpu.SemaphoreType.DMA
    shapes = (
        jax.ShapeDtypeStruct((2, 1, BLK, N), BF16),
        jax.ShapeDtypeStruct((TAPS, TAPS), F32),
    )
    scratch = [pltpu.VMEM(x.shape, x.dtype) for x in arrays] + [
        pltpu.VMEM((DET, BLK, BLK), BF16),
        pltpu.VMEM((DET, 64, BLK), BF16),
        pltpu.VMEM((DET, 64, BLK), BF16),
        pltpu.VMEM((DET, 2, BLK, BLK), BF16),
        pltpu.VMEM((RADIX, BLK, 2 * SUB), BF16),
        pltpu.VMEM((RADIX, BLK, 2 * SUB), F32),
        pltpu.VMEM((RADIX, BLK, 2 * SUB), F32),
        pltpu.VMEM((RADIX, BLK, 2 * SUB), F32),
        pltpu.VMEM((DET, 2, BLK, BLK), BF16),
        pltpu.VMEM((DET, 2, BLK, BLK), BF16),
        pltpu.VMEM((DET, 2, BLK, BLK), BF16),
        pltpu.VMEM((DET, 2, BLK, BLK), BF16),
        pltpu.VMEM((2 * BLK, N), BF16),
        pltpu.VMEM((BLK, N), BF16),
        pltpu.VMEM((RADIX, BLK, SUB), BF16),
        pltpu.VMEM((2, BLK, N // 2), BF16),
        pltpu.VMEM((BLK, N), BF16),
        pltpu.VMEM((BLK, 2 * BLK), F32),
        pltpu.VMEM((1, 32, BLK), F32),
        pltpu.VMEM((frames, 32, BLK), F32),
        pltpu.VMEM((1, 32, BLK), F32),
        pltpu.VMEM((DET, 32, BLK), F32),
        sem((len(arrays),)),
    ]
    scratch += [sem((1, DET))] * 4 + [sem((PARTS, DET))] * 4
    scratch += [sem((frames,))] * 2 + [sem((1, DET))] * 2
    results = pl.pallas_call(
        functools.partial(kernel_body, frames),
        out_shape=shapes,
        in_specs=[pl.BlockSpec(memory_space=pltpu.SMEM)] + [hbm] * len(arrays),
        out_specs=(vmem, vmem),
        scratch_shapes=scratch,
        compiler_params=pltpu.CompilerParams(
            collective_id=0, has_side_effects=True, vmem_limit_bytes=60 * 1024 * 1024
        ),
        cost_estimate=pl.CostEstimate(flops=6_000_000_000, bytes_accessed=16_000_000, transcendentals=0),
    )(positions, *arrays)
    return pl.pallas_call(
        hand_over,
        out_shape=shapes,
        in_specs=[vmem] * 2,
        out_specs=(hbm, hbm),
        scratch_shapes=[sem((2,))],
    )(*results)


def solution(mesh):
    frames = mesh.shape["frames"]
    placed = (
        P(None, "det", None),
        P(None, "det", None),
        P("frames"),
        P("frames", "det", None),
        P(),
    )
    return jax.shard_map(
        functools.partial(on_device, frames),
        mesh=mesh,
        in_specs=placed,
        out_specs=(P(None, "frames", "det", None), P()),
        check_vma=False,
    )
```

```python
import functools
import math

import jax
import jax.numpy as jnp
import ml_dtypes
import numpy as np
from jax import lax
from jax.experimental import pallas as pl
from jax.experimental.pallas import tpu as pltpu
from jax.sharding import PartitionSpec as P

MESH = pl.DeviceIdType.MESH
F32, BF16 = jnp.float32, jnp.bfloat16
N = 2048
HK = 28
TAPS = 2 * HK + 1
RADIX = 8
SUB = N // RADIX
BLK = 128
DET = N // BLK
SPLIT = ((0, 64), (64, 64))
PARTS = len(SPLIT)
ROOT_HALF = math.sqrt(0.5)


def as_bf16(values):
    return np.asarray(values, np.float32).astype(ml_dtypes.bfloat16)


LOADED = (
    "cotangent", "pick", "object", "probe", "inverse", "taps", "kernel_x", "across",
    "forward", "row_lags", "across_back", "spread", "across_own", "lag_x", "eye",
)


@functools.cache
def tables():
    residue = np.arange(RADIX)[:, None, None]
    point = np.arange(SUB)[None, :, None]
    freq = np.arange(SUB)[None, None, :]
    angle = 2 * np.pi * (point * (RADIX * freq + residue) % N) / N
    cos, sin = np.cos(angle) / math.sqrt(N), np.sin(angle) / math.sqrt(N)
    forward = np.concatenate(
        [np.concatenate([cos, -sin], 2), np.concatenate([sin, cos], 2)], 1
    )
    inverse = np.swapaxes(forward, 1, 2)

    spread = np.zeros((1024, 1024))
    for r in range(RADIX):
        spread[RADIX * np.arange(BLK) + r, BLK * r + np.arange(BLK)] = 1

    lag = np.arange(64)
    ky = RADIX * np.arange(SUB)[None, :, None] + residue
    beta = 2 * np.pi * (ky * (lag[None, None, :] - HK) % N) / N
    used = (lag < TAPS)[None, None, :]
    cos, sin = np.cos(beta) * used, np.sin(beta) * used
    row_lags = np.concatenate(
        [np.concatenate([cos, -sin], 2), np.concatenate([sin, cos], 2)], 1
    )

    alpha = 2 * np.pi * (np.arange(BLK) + 0.5) / 256
    lane = np.arange(64)
    halo_u = np.where(lane < HK, lane, lane - HK + HK + BLK)
    halo_on = lane < 2 * HK
    u = np.concatenate([np.arange(BLK) + HK, halo_u, halo_u])
    on = np.concatenate([np.ones(BLK, bool), halo_on, halo_on])
    phase = alpha[:, None] * u[None, :]
    across = np.concatenate([np.cos(phase) * on, -np.sin(phase) * on], 0) / 16

    order = (RADIX * np.arange(16)[None, :] + np.arange(RADIX)[:, None]).reshape(-1)
    phase = alpha[:, None] * (order + HK)[None, :]
    across_own = np.concatenate([np.cos(phase), -np.sin(phase)], 0) / 16
    across_back = 2 * across_own.T

    pick = np.zeros((512, BLK))
    t = np.arange(HK)
    pick[BLK - HK + t, t] = 1
    pick[BLK + t, HK + t] = 1
    pick[256 + BLK - HK + t, 64 + t] = 1
    pick[384 + t, 64 + HK + t] = 1

    tap = np.arange(BLK)
    phase = alpha[:, None] * (tap - HK)[None, :]
    on = tap < TAPS
    kernel_x = np.concatenate([np.cos(phase) * on, np.sin(phase) * on], 1)
    tap = np.arange(BLK) % 64
    phase = alpha[:, None] * (tap - HK)[None, :]
    on = tap < TAPS
    lag_x = 2 * np.stack([np.cos(phase) * on, np.sin(phase) * on])
    return dict(
        forward=as_bf16(forward),
        inverse=as_bf16(inverse),
        spread=as_bf16(spread),
        row_lags=as_bf16(row_lags),
        across=as_bf16(across),
        across_own=as_bf16(across_own),
        across_back=as_bf16(across_back),
        pick=as_bf16(pick),
        eye=as_bf16(np.eye(BLK)),
        kernel_x=kernel_x.astype(np.float32),
        lag_x=lag_x.astype(np.float32),
    )


def dot(a, b):
    return jnp.dot(a, b, preferred_element_type=F32)


def dot_t(a, b):
    return lax.dot_general(a, b, (((1,), (1,)), ((), ())), preferred_element_type=F32)


def add(a, b):
    return (a[0] + b[0], a[1] + b[1])


def sub(a, b):
    return (a[0] - b[0], a[1] - b[1])


def dft4(z, sign):
    c0, c1 = add(z[0], z[2]), sub(z[0], z[2])
    d0, t = add(z[1], z[3]), sub(z[1], z[3])
    d1 = (-t[1], t[0]) if sign > 0 else (t[1], -t[0])
    return [add(c0, d0), add(c1, d1), sub(c0, d0), sub(c1, d1)]


def dft8(z, sign):
    a = [add(z[q], z[q + 4]) for q in range(4)]
    b = [sub(z[q], z[q + 4]) for q in range(4)]
    if sign > 0:
        b[1] = (ROOT_HALF * (b[1][0] - b[1][1]), ROOT_HALF * (b[1][1] + b[1][0]))
        b[2] = (-b[2][1], b[2][0])
        b[3] = (-ROOT_HALF * (b[3][0] + b[3][1]), ROOT_HALF * (b[3][0] - b[3][1]))
    else:
        b[1] = (ROOT_HALF * (b[1][0] + b[1][1]), ROOT_HALF * (b[1][1] - b[1][0]))
        b[2] = (b[2][1], -b[2][0])
        b[3] = (ROOT_HALF * (b[3][1] - b[3][0]), -ROOT_HALF * (b[3][1] + b[3][0]))
    even, odd = dft4(a, sign), dft4(b, sign)
    return [half for pair in zip(even, odd) for half in pair]


def split_residues(source, target, start=0, count=BLK):
    def body(step, carry):
        rows = pl.ds(pl.multiple_of(start + step * 16, 16), 16)
        for p in range(2):
            z = [
                tuple(source[2 * q + p, c, rows, :].astype(F32) for c in range(2))
                for q in range(RADIX)
            ]
            out = dft8(z, -1)
            for r in range(RADIX):
                for c in range(2):
                    first = c * SUB + p * BLK
                    target[r, rows, first : first + BLK] = out[r][c].astype(BF16)
        return carry

    lax.fori_loop(0, count // 16, body, 0)


def join_residues(source, store, start=0, count=BLK):
    def body(step, carry):
        rows = pl.ds(pl.multiple_of(start + step * 16, 16), 16)
        for p in range(2):
            z = [
                tuple(
                    source[r, rows, c * SUB + p * BLK : c * SUB + (p + 1) * BLK]
                    for c in range(2)
                )
                for r in range(RADIX)
            ]
            out = dft8(z, 1)
            for q in range(RADIX):
                for c in range(2):
                    store(2 * q + p, c, start + step * 16, out[q][c].astype(BF16))
        return carry

    lax.fori_loop(0, count // 16, body, 0)


def loop(count, body, unroll=1):
    def step(index, carry):
        for part in range(unroll):
            body(index * unroll + part)
        return carry

    lax.fori_loop(0, count // unroll, step, 0)


def kernel_body(
    frames,
    pos_ref, *refs,
):
    me = lax.axis_index("det")
    my_frame = lax.axis_index("frames")
    count = len(LOADED)
    sources, (wave_ref, kgrad_ref), held = refs[:count], refs[count : count + 2], refs[count + 2 :]
    held, rest = held[:count], held[count:]
    (
        cot_ref, pick_ref, object_ref, probe_ref, inv, taps_ref, kx_ref, across_ref,
        fwd, lags, back_ref, spread, own_ref, lagx_ref, eye_ref,
    ) = held
    (
        cot_main, cot_halo, halo_out, wide, parts, sums, chat,
        spec, half_out, half_in, back_out, back_in,
        ig_x, ig_nat, ig_perm, inten, inten_nat, tap_pad,
        kg_own, kg_frames, kg_sum, kg_det,
        load_sem, main_send, main_recv, halo_send, halo_recv,
        half_send, half_recv, back_send, back_recv,
        kgf_send, kgf_recv, kgd_send, kgd_recv,
    ) = rest

    def det_peer(offset):
        return lax.rem(me + offset, DET)

    def frame_peer(offset):
        return lax.rem(my_frame + offset, frames)

    loads = {
        name: pltpu.make_async_copy(source, target, load_sem.at[index])
        for index, (name, source, target) in enumerate(zip(LOADED, sources, held))
    }
    loads[LOADED[0]].start()

    barrier = pltpu.get_barrier_semaphore()
    loop(DET - 1, lambda o: pl.semaphore_signal(
        barrier, inc=1, device_id={"det": det_peer(o + 1)}, device_id_type=MESH))
    if frames > 1:
        loop(frames - 1, lambda o: pl.semaphore_signal(
            barrier, inc=1, device_id={"frames": frame_peer(o + 1)}, device_id_type=MESH))
    for name in LOADED[1:]:
        loads[name].start()

    def ready(*names):
        for name in names:
            loads[name].wait()


    def exchange(source, target, send, recv, part=0):
        def copy(to, slot):
            return pltpu.make_async_remote_copy(
                src_ref=source(to),
                dst_ref=target(slot),
                send_sem=send.at[part, to],
                recv_sem=recv.at[part, slot],
                device_id={"det": to},
                device_id_type=MESH,
            )

        def start():
            loop(DET - 1, lambda o: copy(det_peer(o + 1), me).start())

        def wait_recv():
            loop(DET - 1, lambda o: copy(det_peer(o + 1), det_peer(o + 1)).wait_recv())

        def wait_send():
            loop(DET - 1, lambda o: copy(det_peer(o + 1), me).wait_send())

        return start, wait_recv, wait_send

    def lanes(block, width=BLK):
        return pl.ds(pl.multiple_of(block * width, width), width)

    def by_parts(source, target, send, recv):
        return [
            exchange(
                lambda t, cut=pl.ds(*cut): source.at[t, :, cut, :],
                lambda t, cut=pl.ds(*cut): target.at[t, :, cut, :],
                send, recv, k,
            )
            for k, cut in enumerate(SPLIT)
        ]

    main = exchange(
        lambda t: cot_ref.at[0, :, lanes(t)], lambda t: cot_main.at[t], main_send, main_recv
    )
    halo = exchange(lambda t: halo_out.at[t], lambda t: cot_halo.at[t], halo_send, halo_recv)
    half = by_parts(half_out, half_in, half_send, half_recv)
    back = by_parts(back_out, back_in, back_send, back_recv)

    def pack(block):
        before = lanes(lax.rem(block + DET - 1, DET))
        after = lanes(lax.rem(block + 1, DET))
        edges = jnp.concatenate(
            [
                cot_ref[0, rows, side]
                for rows in (pl.ds(0, 64), pl.ds(64, 64))
                for side in (before, after)
            ],
            axis=1,
        )
        halo_out[block] = dot(edges, pick_ref[...]).astype(BF16)

    ready("cotangent")
    pl.semaphore_wait(barrier, DET - 1 + frames - 1)
    main[0]()
    ready("pick")
    loop(DET, pack, RADIX)
    halo[0]()

    position = pos_ref[0]
    distance = lax.broadcasted_iota(jnp.int32, (512, 256), 0) - lax.broadcasted_iota(
        jnp.int32, (512, 256), 1
    )
    shift = jnp.where(distance == position, 1.0, 0.0).astype(BF16)

    def exit_wave(q):
        wide_lanes = pl.ds(pl.multiple_of(q * 256, 256), 512)
        own = lanes(q, 256)
        w_re = dot(object_ref[0, :, wide_lanes], shift)
        w_im = dot(object_ref[1, :, wide_lanes], shift)
        p_re, p_im = probe_ref[0, :, own].astype(F32), probe_ref[1, :, own].astype(F32)
        re = (p_re * w_re - p_im * w_im).astype(BF16)
        im = (p_re * w_im + p_im * w_re).astype(BF16)
        for p in range(2):
            wide[2 * q + p, 0] = re[:, p * BLK : (p + 1) * BLK]
            wide[2 * q + p, 1] = im[:, p * BLK : (p + 1) * BLK]

    ready("object", "probe")
    loop(RADIX, exit_wave, RADIX)
    split_residues(wide, parts)
    ready("inverse")

    def first_pass(r):
        out = dot_t(inv[r], parts[r]).astype(BF16).reshape(2, DET, 16, BLK)
        half_out[:, 0, lanes(r, 16), :] = out[0]
        half_out[:, 1, lanes(r, 16), :] = out[1]

    for k in range(PARTS):
        for r in range(SPLIT[k][0] // 16, sum(SPLIT[k]) // 16):
            first_pass(r)
        if k == 0:
            main[2]()
            halo[2]()
        half[k][0]()
    half_in[me] = half_out[me]

    ready("taps", "kernel_x")
    tap_pad[...] = jnp.zeros_like(tap_pad)
    rounded = taps_ref[...].astype(BF16).astype(F32)
    tap_pad[0:TAPS, 0:TAPS] = rounded
    tap_pad[64 : 64 + TAPS, BLK : BLK + TAPS] = rounded
    tap_x = lax.dot_general(
        kx_ref[...], tap_pad[...], (((1,), (1,)), ((), ())),
        precision=lax.Precision.HIGHEST, preferred_element_type=F32,
    )
    tap_hi = tap_x.astype(BF16)
    tap_lo = (tap_x - tap_hi.astype(F32)).astype(BF16)

    cot_main[me] = cot_ref[0, :, lanes(me)]
    cot_halo[me] = halo_out[me]
    ready("across", "forward", "row_lags", "across_back", "spread", "across_own", "lag_x", "eye")
    main[1]()
    halo[1]()
    low = lax.broadcasted_iota(jnp.int32, (64, BLK), 1) < 64

    def cot_across(j):
        edge = cot_halo[j]
        zero = jnp.zeros_like(edge)
        spread_edge = jnp.concatenate(
            [jnp.where(low, edge, zero), jnp.where(low, zero, edge)], axis=0
        )
        both = jnp.concatenate([cot_main[j], spread_edge], axis=1)
        out = dot_t(across_ref[...], both).astype(BF16)
        wide[j, 0] = out[:BLK]
        wide[j, 1] = out[BLK:]

    loop(DET, cot_across, RADIX)
    split_residues(wide, parts)

    def smooth(s):
        c = dot(parts[s], fwd[s])
        chat[s] = c
        k = dot_t(tap_hi, lags[s]) + dot_t(tap_lo, lags[s])
        c_re, c_im, k_re, k_im = c[:, :SUB], c[:, SUB:], k[:, :SUB], k[:, SUB:]
        g = jnp.concatenate(
            [c_re * k_re - c_im * k_im, c_re * k_im + c_im * k_re], axis=1
        )
        sums[s] = dot(g.astype(BF16), inv[s])

    loop(RADIX, smooth, RADIX)

    def store_ig(block, c, row, value):
        rows = pl.ds(pl.multiple_of(c * BLK + row, 16), 16)
        ig_x[rows, block * BLK : (block + 1) * BLK] = value

    join_residues(sums, store_ig)

    def ig_across(b):
        ig_nat[:, lanes(b, 256)] = dot(back_ref[...], ig_x[:, lanes(b, 256)]).astype(BF16)

    loop(RADIX, ig_across, RADIX)
    for h in range(2):

        def to_residues(b, h=h):
            out = dot(ig_nat[:, h * 1024 : (h + 1) * 1024], spread[:, lanes(b, 256)])
            for p in range(2):
                ig_perm[2 * b + p, :, h * BLK : (h + 1) * BLK] = out[
                    :, p * BLK : (p + 1) * BLK
                ].astype(BF16)

        loop(4, to_residues, 4)

    def spectrum(r, rows):
        x = dot(parts[r, rows, :], fwd[r])
        re, im = x[:, :SUB], x[:, SUB:]
        intensity = (re * re + im * im).astype(BF16)
        for h in range(2):
            inten[h, rows, r * BLK : (r + 1) * BLK] = intensity[:, h * BLK : (h + 1) * BLK]
        spec[r, rows, :] = x

    def gradient(r, rows):
        x = spec[r, rows, :]
        re, im = x[:, :SUB], x[:, SUB:]
        twice = 2.0 * ig_perm[r, rows, :].astype(F32)
        grad = jnp.concatenate([(twice * re).astype(BF16), (twice * im).astype(BF16)], axis=1)
        sums[r, rows, :] = dot(grad, inv[r])

    def store_back(block, c, row, value):
        rows = pl.ds(pl.multiple_of(row, 16), 16)
        back_out[block, c, rows, :] = value

    def send_back(k):
        for r in range(RADIX):
            gradient(r, slice(SPLIT[k][0], sum(SPLIT[k])))
        join_residues(sums, store_back, *SPLIT[k])
        back[k][0]()

    for k in range(PARTS):
        half[k][1]()
        split_residues(half_in, parts, *SPLIT[k])
        for r in range(RADIX):
            spectrum(r, slice(SPLIT[k][0], sum(SPLIT[k])))
        if k < PARTS - 1:
            send_back(k)

    for h in range(2):

        def to_natural(b, h=h):
            out = dot_t(inten[h], spread[lanes(b, 256), :]).astype(BF16)
            inten_nat[:, pl.ds(pl.multiple_of(h * 1024 + b * 256, 256), 256)] = out

        loop(4, to_natural, 4)

    def inten_across(b):
        out = dot(own_ref[...], inten_nat[:, lanes(b, 256)]).astype(BF16)
        for p in range(2):
            for c in range(2):
                wide[2 * b + p, c] = out[c * BLK : (c + 1) * BLK, p * BLK : (p + 1) * BLK]

    loop(RADIX, inten_across, RADIX)
    split_residues(wide, parts)

    def lag_sums(s, total):
        x = dot(parts[s], fwd[s])
        c = chat[s]
        x_re, x_im, c_re, c_im = x[:, :SUB], x[:, SUB:], c[:, :SUB], c[:, SUB:]
        product = jnp.concatenate(
            [x_re * c_re + x_im * c_im, x_im * c_re - x_re * c_im], axis=1
        )
        return total + dot(product.astype(BF16), lags[s])

    by_lag = jnp.zeros((BLK, BLK), F32)
    for s in range(RADIX):
        by_lag = lag_sums(s, by_lag)
    by_lag = by_lag.T
    kg = sum(
        lax.dot_general(
            by_lag[c * 64 : (c + 1) * 64], lagx_ref[c], (((1,), (0,)), ((), ())),
            precision=lax.Precision.HIGHEST, preferred_element_type=F32,
        )
        for c in range(2)
    ) * (1.0 / (frames * N))
    first = lax.broadcasted_iota(jnp.int32, (32, BLK), 1) < 64
    kg_own[0] = jnp.where(first, kg[:32], kg[32:])

    def over_frames(source, target, send, recv):
        def copy(to, slot):
            return pltpu.make_async_remote_copy(
                src_ref=source(to),
                dst_ref=target.at[slot],
                send_sem=send.at[to],
                recv_sem=recv.at[slot],
                device_id={"frames": to},
                device_id_type=MESH,
            )

        def start():
            loop(frames - 1, lambda o: copy(frame_peer(o + 1), my_frame).start())

        def wait_recv():
            loop(frames - 1, lambda o: copy(frame_peer(o + 1), frame_peer(o + 1)).wait_recv())

        def wait_send():
            loop(frames - 1, lambda o: copy(frame_peer(o + 1), my_frame).wait_send())

        return start, wait_recv, wait_send

    across_frames = over_frames(lambda f: kg_own.at[0], kg_frames, kgf_send, kgf_recv)
    over_det = exchange(lambda t: kg_sum.at[0], lambda t: kg_det.at[t], kgd_send, kgd_recv)
    across_frames[0]()
    kg_frames[my_frame] = kg_own[0]
    send_back(PARTS - 1)
    back_in[me] = back_out[me]
    across_frames[1]()
    kg_sum[0] = sum(kg_frames[f] for f in range(frames))
    over_det[0]()
    kg_det[me] = kg_sum[0]

    def last_pass(r):
        turned = [
            dot_t(eye_ref[...], back_in[:, c, lanes(r, 16), :].reshape(SUB, BLK)).astype(BF16)
            for c in range(2)
        ]
        sums[r] = dot(jnp.concatenate(turned, axis=1), inv[r])

    for k in range(PARTS):
        back[k][1]()
        for r in range(SPLIT[k][0] // 16, sum(SPLIT[k]) // 16):
            last_pass(r)

    def store_wave(block, c, row, value):
        rows = pl.ds(pl.multiple_of(row, 16), 16)
        wave_ref[c, 0, rows, block * BLK : (block + 1) * BLK] = value

    join_residues(sums, store_wave)

    over_det[1]()
    total = sum(kg_det[j] for j in range(DET))
    kgrad_ref[0:32, :] = total[:, 0:TAPS]
    kgrad_ref[32:TAPS, :] = pltpu.roll(total, 64, 1)[0 : TAPS - 32, 0:TAPS]

    for kind in (*half, *back, across_frames, over_det):
        kind[2]()


def hand_over(wave_in, kgrad_in, wave_out, kgrad_out, wave, kgrad, sems):
    pairs = [(kgrad_in, kgrad, kgrad_out)]
    for c in range(2):
        for first in range(0, BLK, 64):
            at = (c, 0, pl.ds(first, 64))
            pairs.append((wave_in.at[at], wave.at[at], wave_out.at[at]))
    loads = [pltpu.make_async_copy(a, b, sems.at[0, i]) for i, (a, b, _) in enumerate(pairs)]
    stores = [pltpu.make_async_copy(b, c, sems.at[1, i]) for i, (_, b, c) in enumerate(pairs)]
    for load in loads:
        load.start()
    for load, store in zip(loads, stores):
        load.wait()
        store.start()
    for store in stores:
        store.wait()


def on_device(frames, probe, object_field, positions, cotangent, kernel):
    vmem = pl.BlockSpec(memory_space=pltpu.VMEM)
    hbm = pl.BlockSpec(memory_space=pl.ANY)
    arrays = dict(
        tables(), cotangent=cotangent, object=object_field, probe=probe, taps=kernel
    )
    arrays = [arrays[name] for name in LOADED]
    sem = pltpu.SemaphoreType.DMA
    shapes = (
        jax.ShapeDtypeStruct((2, 1, BLK, N), BF16),
        jax.ShapeDtypeStruct((TAPS, TAPS), F32),
    )
    scratch = [pltpu.VMEM(x.shape, x.dtype) for x in arrays] + [
        pltpu.VMEM((DET, BLK, BLK), BF16),
        pltpu.VMEM((DET, 64, BLK), BF16),
        pltpu.VMEM((DET, 64, BLK), BF16),
        pltpu.VMEM((DET, 2, BLK, BLK), BF16),
        pltpu.VMEM((RADIX, BLK, 2 * SUB), BF16),
        pltpu.VMEM((RADIX, BLK, 2 * SUB), F32),
        pltpu.VMEM((RADIX, BLK, 2 * SUB), F32),
        pltpu.VMEM((RADIX, BLK, 2 * SUB), F32),
        pltpu.VMEM((DET, 2, BLK, BLK), BF16),
        pltpu.VMEM((DET, 2, BLK, BLK), BF16),
        pltpu.VMEM((DET, 2, BLK, BLK), BF16),
        pltpu.VMEM((DET, 2, BLK, BLK), BF16),
        pltpu.VMEM((2 * BLK, N), BF16),
        pltpu.VMEM((BLK, N), BF16),
        pltpu.VMEM((RADIX, BLK, SUB), BF16),
        pltpu.VMEM((2, BLK, N // 2), BF16),
        pltpu.VMEM((BLK, N), BF16),
        pltpu.VMEM((BLK, 2 * BLK), F32),
        pltpu.VMEM((1, 32, BLK), F32),
        pltpu.VMEM((frames, 32, BLK), F32),
        pltpu.VMEM((1, 32, BLK), F32),
        pltpu.VMEM((DET, 32, BLK), F32),
        sem((len(arrays),)),
    ]
    scratch += [sem((1, DET))] * 4 + [sem((PARTS, DET))] * 4
    scratch += [sem((frames,))] * 2 + [sem((1, DET))] * 2
    results = pl.pallas_call(
        functools.partial(kernel_body, frames),
        out_shape=shapes,
        in_specs=[pl.BlockSpec(memory_space=pltpu.SMEM)] + [hbm] * len(arrays),
        out_specs=(vmem, vmem),
        scratch_shapes=scratch,
        compiler_params=pltpu.CompilerParams(
            collective_id=0, has_side_effects=True, vmem_limit_bytes=60 * 1024 * 1024
        ),
        cost_estimate=pl.CostEstimate(flops=6_000_000_000, bytes_accessed=16_000_000, transcendentals=0),
    )(positions, *arrays)
    return pl.pallas_call(
        hand_over,
        out_shape=shapes,
        in_specs=[hbm] * 2,
        out_specs=(hbm, hbm),
        scratch_shapes=[
            pltpu.VMEM(shapes[0].shape, BF16),
            pltpu.VMEM(shapes[1].shape, F32),
            sem((2, 5)),
        ],
        compiler_params=pltpu.CompilerParams(vmem_limit_bytes=60 * 1024 * 1024),
    )(*results)


def solution(mesh):
    frames = mesh.shape["frames"]
    placed = (
        P(None, "det", None),
        P(None, "det", None),
        P("frames"),
        P("frames", "det", None),
        P(),
    )
    return jax.shard_map(
        functools.partial(on_device, frames),
        mesh=mesh,
        in_specs=placed,
        out_specs=(P(None, "frames", "det", None), P()),
        check_vma=False,
    )
```

```python
import functools
import math

import jax
import jax.numpy as jnp
import ml_dtypes
import numpy as np
from jax import lax
from jax.experimental import pallas as pl
from jax.experimental.pallas import tpu as pltpu
from jax.sharding import PartitionSpec as P

MESH = pl.DeviceIdType.MESH
F32, BF16 = jnp.float32, jnp.bfloat16
N = 2048
HK = 28
TAPS = 2 * HK + 1
RADIX = 8
SUB = N // RADIX
BLK = 128
DET = N // BLK
SPLIT = ((0, 64), (64, 64))
PARTS = len(SPLIT)
ROOT_HALF = math.sqrt(0.5)


def as_bf16(values):
    return np.asarray(values, np.float32).astype(ml_dtypes.bfloat16)


LOADED = (
    "cotangent", "pick", "object", "probe", "inverse", "taps", "kernel_x", "across",
    "forward", "row_lags", "across_back", "spread", "across_own", "lag_x", "eye",
)


@functools.cache
def tables():
    residue = np.arange(RADIX)[:, None, None]
    point = np.arange(SUB)[None, :, None]
    freq = np.arange(SUB)[None, None, :]
    angle = 2 * np.pi * (point * (RADIX * freq + residue) % N) / N
    cos, sin = np.cos(angle) / math.sqrt(N), np.sin(angle) / math.sqrt(N)
    forward = np.concatenate(
        [np.concatenate([cos, -sin], 2), np.concatenate([sin, cos], 2)], 1
    )
    inverse = np.swapaxes(forward, 1, 2)

    spread = np.zeros((1024, 1024))
    for r in range(RADIX):
        spread[RADIX * np.arange(BLK) + r, BLK * r + np.arange(BLK)] = 1

    lag = np.arange(64)
    ky = RADIX * np.arange(SUB)[None, :, None] + residue
    beta = 2 * np.pi * (ky * (lag[None, None, :] - HK) % N) / N
    used = (lag < TAPS)[None, None, :]
    cos, sin = np.cos(beta) * used, np.sin(beta) * used
    row_lags = np.concatenate(
        [np.concatenate([cos, -sin], 2), np.concatenate([sin, cos], 2)], 1
    )

    alpha = 2 * np.pi * (np.arange(BLK) + 0.5) / 256
    lane = np.arange(64)
    halo_u = np.where(lane < HK, lane, lane - HK + HK + BLK)
    halo_on = lane < 2 * HK
    u = np.concatenate([np.arange(BLK) + HK, halo_u, halo_u])
    on = np.concatenate([np.ones(BLK, bool), halo_on, halo_on])
    phase = alpha[:, None] * u[None, :]
    across = np.concatenate([np.cos(phase) * on, -np.sin(phase) * on], 0) / 16

    order = (RADIX * np.arange(16)[None, :] + np.arange(RADIX)[:, None]).reshape(-1)
    phase = alpha[:, None] * (order + HK)[None, :]
    across_own = np.concatenate([np.cos(phase), -np.sin(phase)], 0) / 16
    across_back = 2 * across_own.T

    pick = np.zeros((512, BLK))
    t = np.arange(HK)
    pick[BLK - HK + t, t] = 1
    pick[BLK + t, HK + t] = 1
    pick[256 + BLK - HK + t, 64 + t] = 1
    pick[384 + t, 64 + HK + t] = 1

    tap = np.arange(BLK)
    phase = alpha[:, None] * (tap - HK)[None, :]
    on = tap < TAPS
    kernel_x = np.concatenate([np.cos(phase) * on, np.sin(phase) * on], 1)
    tap = np.arange(BLK) % 64
    phase = alpha[:, None] * (tap - HK)[None, :]
    on = tap < TAPS
    lag_x = 2 * np.stack([np.cos(phase) * on, np.sin(phase) * on])
    return dict(
        forward=as_bf16(forward),
        inverse=as_bf16(inverse),
        spread=as_bf16(spread),
        row_lags=as_bf16(row_lags),
        across=as_bf16(across),
        across_own=as_bf16(across_own),
        across_back=as_bf16(across_back),
        pick=as_bf16(pick),
        eye=as_bf16(np.eye(BLK)),
        kernel_x=kernel_x.astype(np.float32),
        lag_x=lag_x.astype(np.float32),
    )


def dot(a, b):
    return jnp.dot(a, b, preferred_element_type=F32)


def dot_t(a, b):
    return lax.dot_general(a, b, (((1,), (1,)), ((), ())), preferred_element_type=F32)


def add(a, b):
    return (a[0] + b[0], a[1] + b[1])


def sub(a, b):
    return (a[0] - b[0], a[1] - b[1])


def dft4(z, sign):
    c0, c1 = add(z[0], z[2]), sub(z[0], z[2])
    d0, t = add(z[1], z[3]), sub(z[1], z[3])
    d1 = (-t[1], t[0]) if sign > 0 else (t[1], -t[0])
    return [add(c0, d0), add(c1, d1), sub(c0, d0), sub(c1, d1)]


def dft8(z, sign):
    a = [add(z[q], z[q + 4]) for q in range(4)]
    b = [sub(z[q], z[q + 4]) for q in range(4)]
    if sign > 0:
        b[1] = (ROOT_HALF * (b[1][0] - b[1][1]), ROOT_HALF * (b[1][1] + b[1][0]))
        b[2] = (-b[2][1], b[2][0])
        b[3] = (-ROOT_HALF * (b[3][0] + b[3][1]), ROOT_HALF * (b[3][0] - b[3][1]))
    else:
        b[1] = (ROOT_HALF * (b[1][0] + b[1][1]), ROOT_HALF * (b[1][1] - b[1][0]))
        b[2] = (b[2][1], -b[2][0])
        b[3] = (ROOT_HALF * (b[3][1] - b[3][0]), -ROOT_HALF * (b[3][1] + b[3][0]))
    even, odd = dft4(a, sign), dft4(b, sign)
    return [half for pair in zip(even, odd) for half in pair]


def split_residues(source, target, start=0, count=BLK):
    def body(step, carry):
        rows = pl.ds(pl.multiple_of(start + step * 16, 16), 16)
        for p in range(2):
            z = [
                tuple(source[2 * q + p, c, rows, :].astype(F32) for c in range(2))
                for q in range(RADIX)
            ]
            out = dft8(z, -1)
            for r in range(RADIX):
                for c in range(2):
                    first = c * SUB + p * BLK
                    target[r, rows, first : first + BLK] = out[r][c].astype(BF16)
        return carry

    lax.fori_loop(0, count // 16, body, 0)


def join_residues(source, store, start=0, count=BLK):
    def body(step, carry):
        rows = pl.ds(pl.multiple_of(start + step * 16, 16), 16)
        for p in range(2):
            z = [
                tuple(
                    source[r, rows, c * SUB + p * BLK : c * SUB + (p + 1) * BLK]
                    for c in range(2)
                )
                for r in range(RADIX)
            ]
            out = dft8(z, 1)
            for q in range(RADIX):
                for c in range(2):
                    store(2 * q + p, c, start + step * 16, out[q][c].astype(BF16))
        return carry

    lax.fori_loop(0, count // 16, body, 0)


def loop(count, body, unroll=1):
    def step(index, carry):
        for part in range(unroll):
            body(index * unroll + part)
        return carry

    lax.fori_loop(0, count // unroll, step, 0)


def kernel_body(
    frames,
    pos_ref, *refs,
):
    me = lax.axis_index("det")
    my_frame = lax.axis_index("frames")
    count = len(LOADED)
    sources, (wave_ref, kgrad_ref), held = refs[:count], refs[count : count + 2], refs[count + 2 :]
    held, rest = held[:count], held[count:]
    (
        cot_ref, pick_ref, object_ref, probe_ref, inv, taps_ref, kx_ref, across_ref,
        fwd, lags, back_ref, spread, own_ref, lagx_ref, eye_ref,
    ) = held
    (
        cot_main, cot_halo, halo_out, wide, parts, sums, chat,
        spec, half_out, half_in, back_out, back_in,
        ig_x, ig_nat, ig_perm, inten, inten_nat, tap_pad,
        kg_own, kg_frames, kg_sum, kg_det,
        load_sem, main_send, main_recv, halo_send, halo_recv,
        half_send, half_recv, back_send, back_recv,
        kgf_send, kgf_recv, kgd_send, kgd_recv,
    ) = rest

    def det_peer(offset):
        return lax.rem(me + offset, DET)

    def frame_peer(offset):
        return lax.rem(my_frame + offset, frames)

    loads = {
        name: pltpu.make_async_copy(source, target, load_sem.at[index])
        for index, (name, source, target) in enumerate(zip(LOADED, sources, held))
    }
    loads[LOADED[0]].start()

    barrier = pltpu.get_barrier_semaphore()
    loop(DET - 1, lambda o: pl.semaphore_signal(
        barrier, inc=1, device_id={"det": det_peer(o + 1)}, device_id_type=MESH))
    if frames > 1:
        loop(frames - 1, lambda o: pl.semaphore_signal(
            barrier, inc=1, device_id={"frames": frame_peer(o + 1)}, device_id_type=MESH))
    for name in LOADED[1:]:
        loads[name].start()

    def ready(*names):
        for name in names:
            loads[name].wait()


    def exchange(source, target, send, recv, part=0):
        def copy(to, slot):
            return pltpu.make_async_remote_copy(
                src_ref=source(to),
                dst_ref=target(slot),
                send_sem=send.at[part, to],
                recv_sem=recv.at[part, slot],
                device_id={"det": to},
                device_id_type=MESH,
            )

        def start():
            loop(DET - 1, lambda o: copy(det_peer(o + 1), me).start())

        def wait_recv():
            loop(DET - 1, lambda o: copy(det_peer(o + 1), det_peer(o + 1)).wait_recv())

        def wait_send():
            loop(DET - 1, lambda o: copy(det_peer(o + 1), me).wait_send())

        return start, wait_recv, wait_send

    def lanes(block, width=BLK):
        return pl.ds(pl.multiple_of(block * width, width), width)

    def by_parts(source, target, send, recv):
        return [
            exchange(
                lambda t, cut=pl.ds(*cut): source.at[t, :, cut, :],
                lambda t, cut=pl.ds(*cut): target.at[t, :, cut, :],
                send, recv, k,
            )
            for k, cut in enumerate(SPLIT)
        ]

    main = exchange(
        lambda t: cot_ref.at[0, :, lanes(t)], lambda t: cot_main.at[t], main_send, main_recv
    )
    halo = exchange(lambda t: halo_out.at[t], lambda t: cot_halo.at[t], halo_send, halo_recv)
    half = by_parts(half_out, half_in, half_send, half_recv)
    back = by_parts(back_out, back_in, back_send, back_recv)

    def pack(block):
        before = lanes(lax.rem(block + DET - 1, DET))
        after = lanes(lax.rem(block + 1, DET))
        edges = jnp.concatenate(
            [
                cot_ref[0, rows, side]
                for rows in (pl.ds(0, 64), pl.ds(64, 64))
                for side in (before, after)
            ],
            axis=1,
        )
        halo_out[block] = dot(edges, pick_ref[...]).astype(BF16)

    ready("cotangent")
    pl.semaphore_wait(barrier, DET - 1 + frames - 1)
    main[0]()
    ready("pick")
    loop(DET, pack, RADIX)
    halo[0]()

    position = pos_ref[0]
    distance = lax.broadcasted_iota(jnp.int32, (512, 256), 0) - lax.broadcasted_iota(
        jnp.int32, (512, 256), 1
    )
    shift = jnp.where(distance == position, 1.0, 0.0).astype(BF16)

    def exit_wave(q):
        wide_lanes = pl.ds(pl.multiple_of(q * 256, 256), 512)
        own = lanes(q, 256)
        w_re = dot(object_ref[0, :, wide_lanes], shift)
        w_im = dot(object_ref[1, :, wide_lanes], shift)
        p_re, p_im = probe_ref[0, :, own].astype(F32), probe_ref[1, :, own].astype(F32)
        re = (p_re * w_re - p_im * w_im).astype(BF16)
        im = (p_re * w_im + p_im * w_re).astype(BF16)
        for p in range(2):
            wide[2 * q + p, 0] = re[:, p * BLK : (p + 1) * BLK]
            wide[2 * q + p, 1] = im[:, p * BLK : (p + 1) * BLK]

    ready("object", "probe")
    loop(RADIX, exit_wave, RADIX)
    split_residues(wide, parts)
    ready("inverse")

    def first_pass(r):
        out = dot_t(inv[r], parts[r]).astype(BF16).reshape(2, DET, 16, BLK)
        half_out[:, 0, lanes(r, 16), :] = out[0]
        half_out[:, 1, lanes(r, 16), :] = out[1]

    for k in range(PARTS):
        for r in range(SPLIT[k][0] // 16, sum(SPLIT[k]) // 16):
            first_pass(r)
        if k == 0:
            main[2]()
            halo[2]()
        half[k][0]()
    half_in[me] = half_out[me]

    ready("taps", "kernel_x")
    tap_pad[...] = jnp.zeros_like(tap_pad)
    rounded = taps_ref[...].astype(BF16).astype(F32)
    tap_pad[0:TAPS, 0:TAPS] = rounded
    tap_pad[64 : 64 + TAPS, BLK : BLK + TAPS] = rounded
    tap_x = lax.dot_general(
        kx_ref[...], tap_pad[...], (((1,), (1,)), ((), ())),
        precision=lax.Precision.HIGHEST, preferred_element_type=F32,
    )
    tap_hi = tap_x.astype(BF16)
    tap_lo = (tap_x - tap_hi.astype(F32)).astype(BF16)

    cot_main[me] = cot_ref[0, :, lanes(me)]
    cot_halo[me] = halo_out[me]
    ready("across", "forward", "row_lags", "across_back", "spread", "across_own", "lag_x", "eye")
    main[1]()
    halo[1]()
    low = lax.broadcasted_iota(jnp.int32, (64, BLK), 1) < 64

    def cot_across(j):
        edge = cot_halo[j]
        zero = jnp.zeros_like(edge)
        spread_edge = jnp.concatenate(
            [jnp.where(low, edge, zero), jnp.where(low, zero, edge)], axis=0
        )
        both = jnp.concatenate([cot_main[j], spread_edge], axis=1)
        out = dot_t(across_ref[...], both).astype(BF16)
        wide[j, 0] = out[:BLK]
        wide[j, 1] = out[BLK:]

    loop(DET, cot_across, RADIX)
    split_residues(wide, parts)

    def smooth(s):
        c = dot(parts[s], fwd[s])
        chat[s] = c
        k = dot_t(tap_hi, lags[s]) + dot_t(tap_lo, lags[s])
        c_re, c_im, k_re, k_im = c[:, :SUB], c[:, SUB:], k[:, :SUB], k[:, SUB:]
        g = jnp.concatenate(
            [c_re * k_re - c_im * k_im, c_re * k_im + c_im * k_re], axis=1
        )
        sums[s] = dot(g.astype(BF16), inv[s])

    loop(RADIX, smooth, RADIX)

    def store_ig(block, c, row, value):
        rows = pl.ds(pl.multiple_of(c * BLK + row, 16), 16)
        ig_x[rows, block * BLK : (block + 1) * BLK] = value

    join_residues(sums, store_ig)

    def ig_across(b):
        ig_nat[:, lanes(b, 256)] = dot(back_ref[...], ig_x[:, lanes(b, 256)]).astype(BF16)

    loop(RADIX, ig_across, RADIX)
    for h in range(2):

        def to_residues(b, h=h):
            out = dot(ig_nat[:, h * 1024 : (h + 1) * 1024], spread[:, lanes(b, 256)])
            for p in range(2):
                ig_perm[2 * b + p, :, h * BLK : (h + 1) * BLK] = out[
                    :, p * BLK : (p + 1) * BLK
                ].astype(BF16)

        loop(4, to_residues, 4)

    def spectrum(r, rows):
        x = dot(parts[r, rows, :], fwd[r])
        re, im = x[:, :SUB], x[:, SUB:]
        intensity = (re * re + im * im).astype(BF16)
        for h in range(2):
            inten[h, rows, r * BLK : (r + 1) * BLK] = intensity[:, h * BLK : (h + 1) * BLK]
        spec[r, rows, :] = x

    def gradient(r, rows):
        x = spec[r, rows, :]
        re, im = x[:, :SUB], x[:, SUB:]
        twice = 2.0 * ig_perm[r, rows, :].astype(F32)
        grad = jnp.concatenate([(twice * re).astype(BF16), (twice * im).astype(BF16)], axis=1)
        sums[r, rows, :] = dot(grad, inv[r])

    def store_back(block, c, row, value):
        rows = pl.ds(pl.multiple_of(row, 16), 16)
        back_out[block, c, rows, :] = value

    def send_back(k):
        for r in range(RADIX):
            gradient(r, slice(SPLIT[k][0], sum(SPLIT[k])))
        join_residues(sums, store_back, *SPLIT[k])
        back[k][0]()

    for k in range(PARTS):
        half[k][1]()
        split_residues(half_in, parts, *SPLIT[k])
        for r in range(RADIX):
            spectrum(r, slice(SPLIT[k][0], sum(SPLIT[k])))
        if k < PARTS - 1:
            send_back(k)

    for h in range(2):

        def to_natural(b, h=h):
            out = dot_t(inten[h], spread[lanes(b, 256), :]).astype(BF16)
            inten_nat[:, pl.ds(pl.multiple_of(h * 1024 + b * 256, 256), 256)] = out

        loop(4, to_natural, 4)

    def inten_across(b):
        out = dot(own_ref[...], inten_nat[:, lanes(b, 256)]).astype(BF16)
        for p in range(2):
            for c in range(2):
                wide[2 * b + p, c] = out[c * BLK : (c + 1) * BLK, p * BLK : (p + 1) * BLK]

    loop(RADIX, inten_across, RADIX)
    split_residues(wide, parts)

    def lag_sums(s, total):
        x = dot(parts[s], fwd[s])
        c = chat[s]
        x_re, x_im, c_re, c_im = x[:, :SUB], x[:, SUB:], c[:, :SUB], c[:, SUB:]
        product = jnp.concatenate(
            [x_re * c_re + x_im * c_im, x_im * c_re - x_re * c_im], axis=1
        )
        return total + dot(product.astype(BF16), lags[s])

    by_lag = jnp.zeros((BLK, BLK), F32)
    for s in range(RADIX):
        by_lag = lag_sums(s, by_lag)
    by_lag = by_lag.T
    kg = sum(
        lax.dot_general(
            by_lag[c * 64 : (c + 1) * 64], lagx_ref[c], (((1,), (0,)), ((), ())),
            precision=lax.Precision.HIGHEST, preferred_element_type=F32,
        )
        for c in range(2)
    ) * (1.0 / (frames * N))
    first = lax.broadcasted_iota(jnp.int32, (32, BLK), 1) < 64
    kg_own[0] = jnp.where(first, kg[:32], kg[32:])

    def over_frames(source, target, send, recv):
        def copy(to, slot):
            return pltpu.make_async_remote_copy(
                src_ref=source(to),
                dst_ref=target.at[slot],
                send_sem=send.at[to],
                recv_sem=recv.at[slot],
                device_id={"frames": to},
                device_id_type=MESH,
            )

        def start():
            loop(frames - 1, lambda o: copy(frame_peer(o + 1), my_frame).start())

        def wait_recv():
            loop(frames - 1, lambda o: copy(frame_peer(o + 1), frame_peer(o + 1)).wait_recv())

        def wait_send():
            loop(frames - 1, lambda o: copy(frame_peer(o + 1), my_frame).wait_send())

        return start, wait_recv, wait_send

    across_frames = over_frames(lambda f: kg_own.at[0], kg_frames, kgf_send, kgf_recv)
    over_det = exchange(lambda t: kg_sum.at[0], lambda t: kg_det.at[t], kgd_send, kgd_recv)
    across_frames[0]()
    kg_frames[my_frame] = kg_own[0]
    send_back(PARTS - 1)
    back_in[me] = back_out[me]

    def last_pass(r):
        turned = [
            dot_t(eye_ref[...], back_in[:, c, lanes(r, 16), :].reshape(SUB, BLK)).astype(BF16)
            for c in range(2)
        ]
        sums[r] = dot(jnp.concatenate(turned, axis=1), inv[r])

    for k in range(PARTS):
        back[k][1]()
        for r in range(SPLIT[k][0] // 16, sum(SPLIT[k]) // 16):
            last_pass(r)
        if k == PARTS - 2:
            across_frames[1]()
            kg_sum[0] = sum(kg_frames[f] for f in range(frames))
            over_det[0]()
            kg_det[me] = kg_sum[0]

    def store_wave(block, c, row, value):
        rows = pl.ds(pl.multiple_of(row, 16), 16)
        wave_ref[c, 0, rows, block * BLK : (block + 1) * BLK] = value

    join_residues(sums, store_wave)

    over_det[1]()
    total = sum(kg_det[j] for j in range(DET))
    kgrad_ref[0:32, :] = total[:, 0:TAPS]
    kgrad_ref[32:TAPS, :] = pltpu.roll(total, 64, 1)[0 : TAPS - 32, 0:TAPS]

    for kind in (*half, *back, across_frames, over_det):
        kind[2]()


def hand_over(wave_in, kgrad_in, wave_out, kgrad_out, wave, kgrad, sems):
    pairs = [(kgrad_in, kgrad, kgrad_out)]
    for c in range(2):
        for first in range(0, BLK, 64):
            at = (c, 0, pl.ds(first, 64))
            pairs.append((wave_in.at[at], wave.at[at], wave_out.at[at]))
    loads = [pltpu.make_async_copy(a, b, sems.at[0, i]) for i, (a, b, _) in enumerate(pairs)]
    stores = [pltpu.make_async_copy(b, c, sems.at[1, i]) for i, (_, b, c) in enumerate(pairs)]
    for load in loads:
        load.start()
    for load, store in zip(loads, stores):
        load.wait()
        store.start()
    for store in stores:
        store.wait()


def on_device(frames, probe, object_field, positions, cotangent, kernel):
    vmem = pl.BlockSpec(memory_space=pltpu.VMEM)
    hbm = pl.BlockSpec(memory_space=pl.ANY)
    arrays = dict(
        tables(), cotangent=cotangent, object=object_field, probe=probe, taps=kernel
    )
    arrays = [arrays[name] for name in LOADED]
    sem = pltpu.SemaphoreType.DMA
    shapes = (
        jax.ShapeDtypeStruct((2, 1, BLK, N), BF16),
        jax.ShapeDtypeStruct((TAPS, TAPS), F32),
    )
    scratch = [pltpu.VMEM(x.shape, x.dtype) for x in arrays] + [
        pltpu.VMEM((DET, BLK, BLK), BF16),
        pltpu.VMEM((DET, 64, BLK), BF16),
        pltpu.VMEM((DET, 64, BLK), BF16),
        pltpu.VMEM((DET, 2, BLK, BLK), BF16),
        pltpu.VMEM((RADIX, BLK, 2 * SUB), BF16),
        pltpu.VMEM((RADIX, BLK, 2 * SUB), F32),
        pltpu.VMEM((RADIX, BLK, 2 * SUB), F32),
        pltpu.VMEM((RADIX, BLK, 2 * SUB), F32),
        pltpu.VMEM((DET, 2, BLK, BLK), BF16),
        pltpu.VMEM((DET, 2, BLK, BLK), BF16),
        pltpu.VMEM((DET, 2, BLK, BLK), BF16),
        pltpu.VMEM((DET, 2, BLK, BLK), BF16),
        pltpu.VMEM((2 * BLK, N), BF16),
        pltpu.VMEM((BLK, N), BF16),
        pltpu.VMEM((RADIX, BLK, SUB), BF16),
        pltpu.VMEM((2, BLK, N // 2), BF16),
        pltpu.VMEM((BLK, N), BF16),
        pltpu.VMEM((BLK, 2 * BLK), F32),
        pltpu.VMEM((1, 32, BLK), F32),
        pltpu.VMEM((frames, 32, BLK), F32),
        pltpu.VMEM((1, 32, BLK), F32),
        pltpu.VMEM((DET, 32, BLK), F32),
        sem((len(arrays),)),
    ]
    scratch += [sem((1, DET))] * 4 + [sem((PARTS, DET))] * 4
    scratch += [sem((frames,))] * 2 + [sem((1, DET))] * 2
    results = pl.pallas_call(
        functools.partial(kernel_body, frames),
        out_shape=shapes,
        in_specs=[pl.BlockSpec(memory_space=pltpu.SMEM)] + [hbm] * len(arrays),
        out_specs=(vmem, vmem),
        scratch_shapes=scratch,
        compiler_params=pltpu.CompilerParams(
            collective_id=0, has_side_effects=True, vmem_limit_bytes=60 * 1024 * 1024
        ),
        cost_estimate=pl.CostEstimate(flops=6_000_000_000, bytes_accessed=16_000_000, transcendentals=0),
    )(positions, *arrays)
    return pl.pallas_call(
        hand_over,
        out_shape=shapes,
        in_specs=[hbm] * 2,
        out_specs=(hbm, hbm),
        scratch_shapes=[
            pltpu.VMEM(shapes[0].shape, BF16),
            pltpu.VMEM(shapes[1].shape, F32),
            sem((2, 5)),
        ],
        compiler_params=pltpu.CompilerParams(vmem_limit_bytes=60 * 1024 * 1024),
    )(*results)


def solution(mesh):
    frames = mesh.shape["frames"]
    placed = (
        P(None, "det", None),
        P(None, "det", None),
        P("frames"),
        P("frames", "det", None),
        P(),
    )
    return jax.shard_map(
        functools.partial(on_device, frames),
        mesh=mesh,
        in_specs=placed,
        out_specs=(P(None, "frames", "det", None), P()),
        check_vma=False,
    )
```
